32 devices in a mesh: groups: 2 (over y), gx: 4 (over z), gy: 2 (over x), gz: 2 (over core).
Axes of the slice: x: 2, y: 2, z: 4, core: 2. Of those that a mesh axis runs over, the one named last changes fastest.
Arguments:
- members: bfloat16 [64, 16, 32, 256], P('groups', 'gz', 'gx', 'gy'), parts along dimension 0, may hold values from -6 to 6
- obs_value: float32 [4, 4, 2, 256], P(('groups', 'gz'), 'gx', 'gy'), parts along dimension 0, may hold values from -6 to 6
- obs_rinv: float32 [4, 4, 2, 256], P(('groups', 'gz'), 'gx', 'gy'), parts along dimension 0, may hold values from 0.25 to 4
- obs_count: int32 [4, 4, 2], P(('groups', 'gz'), 'gx', 'gy'), parts along dimension 0, may hold values from 32 to 256, as said below
- stencil_cell: int32 [4, 4, 2, 8, 256], P(('groups', 'gz'), 'gx', 'gy'), parts along dimension 0, may hold values from 0 to 8191, as said below
- stencil_weight: float32 [4, 4, 2, 8, 256], P(('groups', 'gz'), 'gx', 'gy'), parts along dimension 0, may hold values from 0 to 1, as said below
- patch_list: int32 [16, 256, 64], P(('groups', 'gx'), 'gy'), parts along dimension 0, may hold values from 0 to 4607
- patch_taper: float32 [16, 256, 64], P(('groups', 'gx'), 'gy'), parts along dimension 0, may hold values from 0.05 to 1
Outputs:
- analysis: bfloat16 [64, 16, 32, 256], P('groups', 'gz', 'gx', 'gy'), parts along dimension 0
The draws below stay inside these ranges and needn't reach their ends.
There are 2 independent parts, one for each index of `groups`. The reference program is written for one: setup_inputs(seed, part) draws one part's arguments, and reference() takes and returns one part's arrays. A program takes and returns all parts, laid end to end along the dimension named above; each array names one. Nothing has to cross between parts.
Inputs may be any that keep to these rules, and one draw needn't show every extreme that they name: Each buffer's first obs_count slots are live; in every draw some buffer is full. `stencil_cell`: the eight corners (l + a, x + b, y + c), a, b, c in 0, 1, of one grid box of the owner's block, as local numbers (l*8 + x)*128 + y. `stencil_weight`: trilinear weights: nonnegative, summing to one over a sample's eight cells. `patch_list`: ids ((h*3 + a)*3 + b)*256 + o into the buffers of both level halves of the 3 x 3 tiles around the patch's own.
All inputs are finite; a program needn't handle non-finite values.
Results may differ from the reference program's by a relative error of at most 0.001.
Values sent between devices are 32-bit elements; how exact they have to be, the bound alone decides.
No kernel may reach another device: no remote copies, remote signals or barrier semaphores. Data moves between devices by JAX's collectives and lax.ppermute only.
A program may use at most 64 MiB of HBM per device.

```python
import math
import jax
import jax.numpy as jnp
import numpy as np
from jax import lax

K = 32
LDEV = 8
CXD = 8
CYD = 128
OCAP = 256
PX = 4
MLOC = 64
STEN = 8
NSIT = 4
LEV = 16
NX = 32
NY = 256
NPX = 8
N_GX = 4
N_GY = 2
N_GZ = 2


def draw_obs_count(key, part):
    key = jax.random.fold_in(key, 13)
    key_one, key_two = jax.random.split(key)
    buffers = N_GZ * N_GX * N_GY
    counts = jax.random.randint(key_one, (buffers,), max(OCAP // 8, 1), OCAP + 1)
    chosen = jax.random.randint(key_two, (), 0, buffers)
    counts = jnp.where(jnp.arange(buffers) == chosen, OCAP, counts)
    return counts.reshape(N_GZ, N_GX, N_GY).astype(jnp.int32)


def draw_stencil_cell(key, part):
    key = jax.random.fold_in(key, 17)
    key_lev, key_x, key_y = jax.random.split(key, 3)
    shape = (N_GZ, N_GX, N_GY, 1, OCAP)
    base_lev = jax.random.randint(key_lev, shape, 0, LDEV - 1)
    base_x = jax.random.randint(key_x, shape, 0, CXD - 1)
    base_y = jax.random.randint(key_y, shape, 0, CYD - 1)
    corner = np.arange(8)
    step_lev = jnp.asarray(corner >> 2 & 1, dtype=jnp.int32).reshape(1, 1, 1, 8, 1)
    step_x = jnp.asarray(corner >> 1 & 1, dtype=jnp.int32).reshape(1, 1, 1, 8, 1)
    step_y = jnp.asarray(corner & 1, dtype=jnp.int32).reshape(1, 1, 1, 8, 1)
    cells = ((base_lev + step_lev) * CXD + base_x + step_x) * CYD + base_y + step_y
    return cells.astype(jnp.int32)


def draw_stencil_weight(key, part):
    key = jax.random.fold_in(key, 19)
    key_lev, key_x, key_y = jax.random.split(key, 3)
    shape = (N_GZ, N_GX, N_GY, 1, OCAP)
    frac_lev = jax.random.uniform(key_lev, shape, jnp.float32)
    frac_x = jax.random.uniform(key_x, shape, jnp.float32)
    frac_y = jax.random.uniform(key_y, shape, jnp.float32)
    corner = np.arange(8)
    pick_lev = jnp.asarray(corner >> 2 & 1, dtype=jnp.float32).reshape(1, 1, 1, 8, 1)
    pick_x = jnp.asarray(corner >> 1 & 1, dtype=jnp.float32).reshape(1, 1, 1, 8, 1)
    pick_y = jnp.asarray(corner & 1, dtype=jnp.float32).reshape(1, 1, 1, 8, 1)
    weight_lev = pick_lev * frac_lev + (1.0 - pick_lev) * (1.0 - frac_lev)
    weight_x = pick_x * frac_x + (1.0 - pick_x) * (1.0 - frac_x)
    weight_y = pick_y * frac_y + (1.0 - pick_y) * (1.0 - frac_y)
    return (weight_lev * weight_x * weight_y).astype(jnp.float32)


def set_ends(array, key, smallest, largest):
    spot = [jax.random.randint(jax.random.fold_in(key, axis), (), 0, length) for axis, length in enumerate(array.shape)]
    main_axis = array.shape.index(max(array.shape))
    neighbour = spot[:main_axis] + [(spot[main_axis] + 1) % array.shape[main_axis]] + spot[main_axis + 1:]
    return array.at[tuple(spot)].set(smallest).at[tuple(neighbour)].set(largest)


def shard_levels(key, dims, pieces, smallest, top_value):
    def one(axis_at, blocks):
        heights = jax.random.uniform(jax.random.fold_in(jax.random.fold_in(key, 6), axis_at), (blocks,), jnp.float32, smallest / len(pieces), top_value / len(pieces))
        return jnp.repeat(jnp.exp(heights), dims[axis_at] // blocks).reshape((-1,) + (1,) * (len(dims) - axis_at - 1))

    loudness = one(*pieces[0])
    for cut in pieces[1:]:
        loudness = loudness * one(*cut)
    return loudness


def bell_draw(rng, shape, spread, bound, pieces=(), kind=jnp.bfloat16):
    array = jax.random.normal(rng, shape, jnp.float32) * spread
    if len(pieces) > 0:
        array = shard_levels(rng, shape, pieces, -0.22, 0.18) * array
    return jnp.clip(array, min=-bound, max=bound).astype(kind)


def setup_inputs(seed: int = 0, part: int = 0) -> dict:
    key_of = jax.random.split(jax.random.key(seed), 9)
    part_splits = jax.random.split(jax.random.fold_in(key_of[8], part), 9)
    members = bell_draw(part_splits[0], (K, LEV, NX, NY), 1.0, 6.0, ((1, 2), (2, 4), (3, 2)))
    obs_value = bell_draw(part_splits[1], (N_GZ, N_GX, N_GY, OCAP), 1.0, 6.0, ((0, 2), (1, 4), (2, 2)), jnp.float32)
    obs_rinv = jnp.clip(jnp.exp(math.log(4.0) - 2.7725887 * jax.random.uniform(part_splits[2], (N_GZ, N_GX, N_GY, OCAP), jnp.float32) ** shard_levels(part_splits[2], (N_GZ, N_GX, N_GY, OCAP), ((0, 2), (1, 4), (2, 2)), -0.2, 0.2)), 0.25, 4.0)
    obs_count = draw_obs_count(jax.random.fold_in(jax.random.fold_in(key_of[8], part), 71), part)
    stencil_cell = draw_stencil_cell(jax.random.fold_in(jax.random.fold_in(key_of[8], part), 71), part)
    stencil_weight = draw_stencil_weight(jax.random.fold_in(jax.random.fold_in(key_of[8], part), 71), part)
    patch_list = set_ends(jax.random.randint(part_splits[6], (NPX, NY, MLOC), 0, 9 * N_GZ * OCAP), jax.random.fold_in(part_splits[6], 1), 0, (9 * N_GZ * OCAP) - 1).astype(jnp.int32)
    patch_taper = jnp.clip(jnp.exp(math.log(1.0) - 2.9957323 * jax.random.uniform(part_splits[7], (NPX, NY, MLOC), jnp.float32) ** shard_levels(part_splits[7], (NPX, NY, MLOC), ((0, 4), (1, 2)), -0.2, 0.2)), 0.05, 1.0)
    return {"members": members, "obs_value": obs_value, "obs_rinv": obs_rinv, "obs_count": obs_count, "stencil_cell": stencil_cell, "stencil_weight": stencil_weight, "patch_list": patch_list, "patch_taper": patch_taper}


def batched_product(first_mat, second_mat):
    return jnp.einsum('ijp,jkp->ikp', first_mat, second_mat, precision=lax.Precision.HIGHEST)

def transforms(nearby, list_ids, tapers):
    ensemble = nearby.shape[0] - 2
    picked = jnp.take(nearby, list_ids.reshape(-1), axis=1).reshape(ensemble + 2, list_ids.shape[0], list_ids.shape[1])
    observed_perturbation = picked[:ensemble]
    innovation = picked[ensemble]
    weight = picked[ensemble + 1] * tapers
    scaled_product = observed_perturbation * weight[None]
    gram_matrix = jnp.einsum('sfe,bfe->sbf', scaled_product, observed_perturbation, precision=lax.Precision.HIGHEST)
    rhs_vec = jnp.einsum('ipm,pm->ip', scaled_product, innovation, precision=lax.Precision.HIGHEST)
    identity = jnp.eye(ensemble, dtype=jnp.float32)[:, :, None]
    system = gram_matrix + (ensemble - 1.0) * identity
    half_trace = 0.5 * jnp.einsum('iip->p', system)
    iterate = system / half_trace[None, None]
    root = jnp.broadcast_to(identity, system.shape)
    for sweep in range(NSIT):
        middle = 1.5 * identity - 0.5 * batched_product(root, iterate)
        iterate = batched_product(iterate, middle)
        root = batched_product(middle, root)
    inner = jnp.einsum('ijp,jp->ip', root, rhs_vec, precision=lax.Precision.HIGHEST)
    mean_weight = jnp.einsum('ijp,jp->ip', root, inner, precision=lax.Precision.HIGHEST) / half_trace[None]
    return mean_weight[:, None, :] + math.sqrt(ensemble - 1.0) * root / jnp.sqrt(half_trace)[None, None]

def make_packet(device_block, values, inverse_var, active_count, cells, weights):
    field = device_block.astype(jnp.float32)
    mean = lax.optimization_barrier(jnp.sum(field, axis=0)) / K
    pert = field - mean[None, :]
    pert_at = jnp.take(pert, cells, axis=1)
    mean_at = jnp.take(mean, cells, axis=0)
    observed_perturbation = lax.optimization_barrier(jnp.sum(pert_at * weights[None], axis=1))
    innovation = values - lax.optimization_barrier(jnp.sum(mean_at * weights, axis=0))
    live = (jnp.arange(OCAP, dtype=jnp.int32) < active_count).astype(jnp.float32)
    return jnp.concatenate([observed_perturbation, innovation[None], (inverse_var * live)[None]], axis=0)

def reference(members, obs_value, obs_rinv, obs_count, stencil_cell, stencil_weight, patch_list, patch_taper):
    devices = N_GZ * N_GX * N_GY
    blocks = members.reshape(K, N_GZ, LDEV, N_GX, CXD, N_GY, CYD)
    blocks = jnp.transpose(blocks, (1, 3, 5, 0, 2, 4, 6)).reshape(devices, K, LDEV * CXD * CYD)

    def packet_of(items):
        return make_packet(items[0], items[1], items[2], items[3], items[4], items[5])
    packets = lax.map(packet_of, (blocks, obs_value.reshape(devices, OCAP), obs_rinv.reshape(devices, OCAP), obs_count.reshape(devices), stencil_cell.reshape(devices, STEN, OCAP), stencil_weight.reshape(devices, STEN, OCAP)))
    packets = packets.reshape(N_GZ, N_GX, N_GY, K + 2, OCAP)
    row_count = CXD // PX
    steps_plus_minus = jnp.arange(-1, 2, dtype=jnp.int32)

    def tile_fn(tile_index):
        tile_x = tile_index // N_GY
        tile_y = tile_index % N_GY
        nearby = jnp.take(packets, (tile_x + steps_plus_minus) % N_GX, axis=1)
        nearby = jnp.take(nearby, (tile_y + steps_plus_minus) % N_GY, axis=2)
        nearby = jnp.transpose(nearby, (3, 0, 1, 2, 4)).reshape(K + 2, -1)
        list_ids = lax.dynamic_slice(patch_list, (tile_x * row_count, tile_y * CYD, jnp.int32(0)), (row_count, CYD, MLOC))
        tapers = lax.dynamic_slice(patch_taper, (tile_x * row_count, tile_y * CYD, jnp.int32(0)), (row_count, CYD, MLOC))
        result = transforms(nearby, list_ids.reshape(-1, MLOC), tapers.reshape(-1, MLOC))
        return result.reshape(K, K, row_count, CYD)
    tiles = lax.map(tile_fn, jnp.arange(N_GX * N_GY, dtype=jnp.int32))
    tiles = tiles.reshape(N_GX, N_GY, K, K, row_count, CYD)
    tiles = jnp.transpose(tiles, (2, 3, 0, 4, 1, 5)).reshape(K, K, NPX, NY)

    def row_update(patch_row):
        columns = lax.dynamic_slice_in_dim(members, patch_row * PX, PX, 2).astype(jnp.float32)
        mean = lax.optimization_barrier(jnp.sum(columns, axis=0)) / K
        pert = columns - mean[None]
        trio = jnp.take(tiles, (patch_row + steps_plus_minus) % NPX, axis=2)
        outputs = []
        for column in range(PX):
            index_shift = (column + 0.5) / PX - 0.5
            beside = trio[:, :, 0] if index_shift < 0 else trio[:, :, 2]
            blend = (1.0 - abs(index_shift)) * trio[:, :, 1] + abs(index_shift) * beside
            update = jnp.einsum('jly,jky->kly', pert[:, :, column], blend, precision=lax.Precision.HIGHEST)
            outputs.append((mean[None, :, column] + update).astype(jnp.bfloat16))
        return jnp.stack(outputs, axis=2)
    rows_out = lax.map(row_update, jnp.arange(NPX, dtype=jnp.int32))
    return jnp.transpose(rows_out, (1, 2, 0, 3, 4)).reshape(K, LEV, NX, NY)
```

```python
import functools
import math

import jax
import jax.numpy as jnp
from jax import lax
from jax.experimental import pallas as pl
from jax.experimental.pallas import tpu as pltpu
from jax.sharding import PartitionSpec as P

PX = 4
F32 = jnp.float32
BF16 = jnp.bfloat16
LANES = 128
SUB = 8
VMEM_LIMIT = 40 << 20


def params():
    return pltpu.CompilerParams(vmem_limit_bytes=VMEM_LIMIT)


def spread(ref, row):
    return ref[pl.ds(row, SUB, stride=0), :]


def block_base(ens):
    nb = ens // SUB
    base, at = [], 0
    for i in range(ens):
        base.append(at)
        at += SUB * (nb - i // SUB)
    return base, at


def observe_kernel(count_ref, members_ref, cell_ref, weight_ref, value_ref, rinv_ref, out_ref, wx, pick, part):
    ens, levels, width_x, width_y = members_ref.shape
    slots = cell_ref.shape[1]
    sten = cell_ref.shape[0]
    cell = cell_ref[...]
    low = jnp.bitwise_and(cell, width_y - 1)
    high = lax.shift_right_logical(cell, width_y.bit_length() - 1)
    low0 = jnp.min(low, axis=0, keepdims=True)
    code = high * 2 + (low - low0)
    weight = weight_ref[...]
    x_iota = lax.broadcasted_iota(jnp.int32, (width_x, slots), 0)
    for level in range(levels):
        for c in range(2):
            want = (level * width_x + x_iota) * 2 + c
            total = jnp.zeros((width_x, slots), F32)
            for s in range(sten):
                total = total + jnp.where(code[s : s + 1] == want, weight[s : s + 1], 0.0)
            wx[c, level * width_x : (level + 1) * width_x, :] = total
    y_iota = lax.broadcasted_iota(jnp.int32, (width_y, slots), 0)
    pick[:, :slots] = jnp.where(y_iota == low0, 1.0, 0.0).astype(BF16)
    pick[:, slots:] = jnp.where(y_iota == low0 + 1, 1.0, 0.0).astype(BF16)

    def member(k, _):
        rows = members_ref[k].astype(F32).reshape(levels * width_x, width_y).astype(BF16)
        got = jnp.dot(rows, pick[...], preferred_element_type=F32)
        term = got[:, :slots] * wx[0] + got[:, slots:] * wx[1]
        total = term[:SUB]
        for q in range(1, levels * width_x // SUB):
            total = total + term[q * SUB : (q + 1) * SUB]
        for half in range(slots // LANES):
            part[half, pl.ds(pl.multiple_of(k * SUB, SUB), SUB), :] = total[:, half * LANES : (half + 1) * LANES]
        return 0

    lax.fori_loop(0, ens, member, 0, unroll=2)
    groups = []
    for kb in range(ens // SUB):
        halves = []
        for half in range(slots // LANES):
            total = part[half, pl.ds(kb * SUB * SUB, SUB, stride=SUB), :]
            for s in range(1, SUB):
                total = total + part[half, pl.ds(kb * SUB * SUB + s, SUB, stride=SUB), :]
            halves.append(total)
        groups.append(jnp.concatenate(halves, axis=1))
    total = groups[0]
    for group in groups[1:]:
        total = total + group
    mean = jnp.sum(total, axis=0, keepdims=True) / ens
    for kb in range(ens // SUB):
        out_ref[kb * SUB : (kb + 1) * SUB, :] = groups[kb] - mean
    live = lax.broadcasted_iota(jnp.int32, (1, slots), 1) < count_ref[0]
    innovation = value_ref[...] - mean
    rinv = jnp.where(live, rinv_ref[...], 0.0)
    row = lax.broadcasted_iota(jnp.int32, (SUB, slots), 0)
    out_ref[ens : ens + SUB, :] = jnp.where(row == 0, innovation, jnp.where(row == 1, rinv, 0.0))


def observe(members, cell, weight, value, rinv, count):
    ens, levels, width_x, width_y = members.shape
    sten, slots = cell.shape
    vmem = pl.BlockSpec(memory_space=pltpu.VMEM)
    return pl.pallas_call(
        observe_kernel,
        out_shape=jax.ShapeDtypeStruct((ens + SUB, slots), F32),
        in_specs=[pl.BlockSpec(memory_space=pltpu.SMEM)] + [vmem] * 5,
        out_specs=vmem,
        scratch_shapes=[
            pltpu.VMEM((2, levels * width_x, slots), F32),
            pltpu.VMEM((width_y, 2 * slots), BF16),
            pltpu.VMEM((slots // LANES, ens * SUB, LANES), F32),
        ],
        compiler_params=params(),
        name="observe",
    )(count, members, cell, weight, value, rinv)


def taper_kernel(gz_ref, own_ref, halo_ref, high_ref, low_ref, code_s, slot_s, taper_s, *, n_x, n_y, slots):
    patches, mloc = own_ref.shape[0], own_ref.shape[1] // 2
    batch = patches // SUB
    gz = gz_ref[0]
    n_buf = 2 * n_x * n_y
    lanes = SUB * mloc
    for r, ref in enumerate((own_ref, halo_ref)):
        shift = 0 if r == 0 else jnp.where(gz == 0, -1, 1)
        pairs = [ref[pl.ds(q, batch, stride=SUB), :] for q in range(SUB)]
        ids = jnp.concatenate([pair[:, :mloc] for pair in pairs], axis=1).astype(jnp.int32)
        taper = jnp.concatenate([pair[:, mloc:] for pair in pairs], axis=1)
        slot = jnp.bitwise_and(ids, slots - 1)
        tile = lax.shift_right_logical(ids, slots.bit_length() - 1)
        upper = (tile >= 9).astype(jnp.int32)
        tile = tile - 9 * upper
        a = (tile >= 3).astype(jnp.int32) + (tile >= 6).astype(jnp.int32)
        b = tile - 3 * a
        other = jnp.where(upper == gz, 0, 1)
        x = lax.rem(a - 1 + shift + 2 * n_x, n_x)
        y = lax.rem(b - 1 + n_y, n_y)
        patch = lax.shift_right_logical(lax.broadcasted_iota(jnp.int32, ids.shape, 1), mloc.bit_length() - 1)
        rows = pl.ds(r * batch, batch)
        code_s[rows, :] = ((other * n_x + x) * n_y + y) * SUB + patch
        slot_s[rows, :] = slot
        taper_s[rows, :] = taper

    def dense(it):
        code = code_s[pl.ds(it, 1), :]
        slot = slot_s[pl.ds(it, 1), :]
        taper = taper_s[pl.ds(it, 1), :]
        hit = lax.broadcasted_iota(jnp.int32, (n_buf * SUB, lanes), 0) == code
        coarse = taper.astype(BF16).astype(F32)
        left = jnp.concatenate(
            [jnp.where(hit, coarse, 0.0).astype(BF16), jnp.where(hit, taper - coarse, 0.0).astype(BF16)], axis=0
        )
        right = jnp.where(lax.broadcasted_iota(jnp.int32, (slots, lanes), 0) == slot, 1.0, 0.0).astype(BF16)
        both = lax.dot_general(left, right, (((1,), (1,)), ((), ())), preferred_element_type=F32)
        return both[: n_buf * SUB] + both[n_buf * SUB :]

    def body(it, _):
        first = dense(2 * it)
        second = dense(2 * it + 1)
        for n in range(n_buf):
            rows = slice(n * SUB, (n + 1) * SUB)
            block = jnp.concatenate([first[rows], second[rows]], axis=0)
            high = block.astype(BF16)
            at = pl.ds(pl.multiple_of(it * 2 * SUB, 2 * SUB), 2 * SUB)
            high_ref[n, at, :] = high
            low_ref[n, at, :] = (block - high.astype(F32)).astype(BF16)
        return 0

    lax.fori_loop(0, batch, body, 0)


def dense_tapers(gz, own, halo, n_x, n_y, slots):
    patches, mloc = own.shape[0], own.shape[1] // 2
    vmem = pl.BlockSpec(memory_space=pltpu.VMEM)
    n_buf = 2 * n_x * n_y
    shape = jax.ShapeDtypeStruct((n_buf, 2 * patches, slots), BF16)
    batch = patches // SUB
    return pl.pallas_call(
        functools.partial(taper_kernel, n_x=n_x, n_y=n_y, slots=slots),
        out_shape=(shape, shape),
        in_specs=[pl.BlockSpec(memory_space=pltpu.SMEM), vmem, vmem],
        out_specs=(vmem, vmem),
        scratch_shapes=[
            pltpu.VMEM((2 * batch, SUB * mloc), jnp.int32),
            pltpu.VMEM((2 * batch, SUB * mloc), jnp.int32),
            pltpu.VMEM((2 * batch, SUB * mloc), F32),
        ],
        compiler_params=params(),
        name="dense_tapers",
    )(gz, own, halo)


def gram_kernel(*refs, ens, n_stack):
    stacks = refs[:n_stack]
    high_ref, low_ref, out_ref, z_s, zr_s = refs[n_stack:]
    nb = ens // SUB
    slots = stacks[0].shape[2]
    base, tri = block_base(ens)
    rows = tri + ens
    nt = (((1,), (1,)), ((), ()))
    first = True
    n = 0
    for stack in stacks:
        for t in range(stack.shape[0]):
            ob = stack[t, :ens, :]
            rinv = stack[t, ens + 1 : ens + 2, :]
            zr_s[...] = ob * rinv
            wi = stack[t, ens : ens + 1, :]
            for i in range(0, ens, 2):
                ib = i // SUB
                part = jnp.concatenate(
                    [ob[kb * SUB : (kb + 1) * SUB] * zr_s[q : q + 1, :] for q in (i, i + 1) for kb in range(ib, nb)], axis=0
                )
                high = part.astype(BF16)
                z_s[base[i] : base[i] + part.shape[0], :] = high
                z_s[rows + base[i] : rows + base[i] + part.shape[0], :] = (part - high.astype(F32)).astype(BF16)
            part = zr_s[...] * wi
            high = part.astype(BF16)
            z_s[tri:rows, :] = high
            z_s[rows + tri : 2 * rows, :] = (part - high.astype(F32)).astype(BF16)
            got = lax.dot_general(z_s[...], high_ref[n], nt, preferred_element_type=F32)
            more = lax.dot_general(z_s[:rows, :], low_ref[n], nt, preferred_element_type=F32)
            total = got[:rows] + (got[rows:] + more)
            out_ref[...] = total if first else out_ref[...] + total
            first = False
            n += 1


def grams(stacks, high, low, ens):
    vmem = pl.BlockSpec(memory_space=pltpu.VMEM)
    _, tri = block_base(ens)
    rows = tri + ens
    patches, slots = high.shape[1:]
    return pl.pallas_call(
        functools.partial(gram_kernel, ens=ens, n_stack=len(stacks)),
        out_shape=jax.ShapeDtypeStruct((rows, patches), F32),
        in_specs=[vmem] * (len(stacks) + 2),
        out_specs=vmem,
        scratch_shapes=[pltpu.VMEM((2 * rows, slots), BF16), pltpu.VMEM((ens, slots), F32)],
        compiler_params=params(),
        name="grams",
    )(*stacks, high, low)


def product(ens, a, b, dests, epilogue):
    nb = ens // SUB
    for ib in range(nb):
        n = nb - ib
        rows = 4 if n > 2 else 8

        def body(step, _, ib=ib, n=n, rows=rows):
            i0 = ib * SUB + step * rows
            acc = [[None] * n for _ in range(rows)]
            for j in range(ens):
                right = [b[j * ens + SUB * kb : j * ens + SUB * (kb + 1), :] for kb in range(ib, nb)]
                for ii in range(rows):
                    left = spread(a, (i0 + ii) * ens + j)
                    for q in range(n):
                        term = left * right[q]
                        acc[ii][q] = term if j == 0 else acc[ii][q] + term
            for ii in range(rows):
                for q in range(n):
                    kb = ib + q
                    eye = None
                    if q == 0:
                        eye = lax.broadcasted_iota(jnp.int32, (SUB, LANES), 0) == step * rows + ii
                    outs = epilogue(acc[ii][q], pl.ds((i0 + ii) * ens + SUB * kb, SUB), eye)
                    for dest, value in zip(dests, outs):
                        dest[pl.ds((i0 + ii) * ens + SUB * kb, SUB), :] = value
                        if kb > ib:
                            dest[pl.ds(SUB * kb * ens + i0 + ii, SUB, stride=ens), :] = value
            return 0

        lax.fori_loop(0, SUB // rows, body, 0)


def root_kernel(gram_ref, out_ref, s_a, s_b, s_c, s_d, vec, *, ens):
    nb = ens // SUB
    base, tri = block_base(ens)
    diag = gram_ref[0:1, :]
    for i in range(1, ens):
        at = base[i] + i % SUB
        diag = diag + gram_ref[at : at + 1, :]
    half = 0.5 * (diag + (ens - 1.0) * ens)
    scale = jnp.broadcast_to(1.0 / half, (SUB, LANES))
    iota = lax.broadcasted_iota(jnp.int32, (SUB, LANES), 0)
    for i in range(ens):
        for kb in range(i // SUB, nb):
            at = base[i] + SUB * (kb - i // SUB)
            value = gram_ref[at : at + SUB, :]
            if kb == i // SUB:
                value = jnp.where(iota == i % SUB, value + (ens - 1.0), value)
            value = value * scale
            s_a[i * ens + SUB * kb : i * ens + SUB * (kb + 1), :] = value
            if kb > i // SUB:
                s_a[pl.ds(SUB * kb * ens + i, SUB, stride=ens), :] = value

    def plain(acc, at, eye):
        return (acc,)

    def quadratic(lin):
        def epilogue(acc, at, eye):
            rest = 0.0625 * acc - 0.5625 * lin[at, :]
            if eye is not None:
                rest = jnp.where(eye, rest + 1.6875, rest)
            return (acc, rest)

        return epilogue

    def quartic(lin):
        def epilogue(acc, at, eye):
            rest = acc - 2.4375 * lin[at, :]
            if eye is not None:
                rest = jnp.where(eye, rest + 2.25, rest)
            return (rest,)

        return epilogue

    product(ens, s_a, s_a, (s_b, s_c), quadratic(s_a))
    product(ens, s_b, s_c, (s_d,), quartic(s_a))
    product(ens, s_d, s_d, (s_b,), plain)
    product(ens, s_a, s_b, (s_c,), plain)
    product(ens, s_c, s_c, (s_a, s_b), quadratic(s_c))
    product(ens, s_a, s_b, (vec.at[pl.ds(0, ens * ens)],), quartic(s_c))
    product(ens, s_d, vec.at[pl.ds(0, ens * ens)], (s_a,), plain)

    right = ens * ens
    vec[right : right + ens, :] = gram_ref[tri : tri + ens, :]

    def apply(source):
        sums = [None] * nb
        for i in range(ens):
            left = spread(vec, source + i)
            for kb in range(nb):
                term = left * s_a[i * ens + SUB * kb : i * ens + SUB * (kb + 1), :]
                sums[kb] = term if i == 0 else sums[kb] + term
        return sums

    inner = apply(right)
    for kb in range(nb):
        vec[right + ens + SUB * kb : right + ens + SUB * (kb + 1), :] = inner[kb]
    outer = apply(right + ens)
    for kb in range(nb):
        out_ref[tri + SUB * kb : tri + SUB * (kb + 1), :] = outer[kb] * scale
    factor = jnp.broadcast_to(math.sqrt(ens - 1.0) / jnp.sqrt(half), (SUB, LANES))
    for i in range(ens):
        for kb in range(i // SUB, nb):
            at = base[i] + SUB * (kb - i // SUB)
            out_ref[at : at + SUB, :] = s_a[i * ens + SUB * kb : i * ens + SUB * (kb + 1), :] * factor


def roots(gram, row, ens):
    rows = gram.shape[0]
    square = pltpu.VMEM((ens * ens, LANES), F32)
    return pl.pallas_call(
        functools.partial(root_kernel, ens=ens),
        out_shape=jax.ShapeDtypeStruct((rows, LANES), F32),
        grid=(1,),
        in_specs=[pl.BlockSpec((rows, LANES), lambda g: (0, row))],
        out_specs=pl.BlockSpec((rows, LANES), lambda g: (0, 0)),
        scratch_shapes=[square] * 4 + [pltpu.VMEM((ens * ens + 2 * ens, LANES), F32)],
        compiler_params=params(),
        name="roots",
    )(gram)


def update_kernel(gz_ref, members_ref, own_ref, pair_ref, halo_ref, far_ref, out_ref, pert_s, mean_s, tx_s):
    ens, levels, width_x, width_y = members_ref.shape
    nb = ens // SUB
    base, tri = block_base(ens)
    column = lax.broadcasted_iota(jnp.int32, (width_x, width_y), 0)
    column = jnp.where(gz_ref[0] == 0, column, width_x - 1 - column).astype(F32)
    place = (column + 0.5) / PX - 0.5
    weights = [
        jnp.maximum(0.0, 1.0 - jnp.abs(place - centre)) for centre in (0.0, 1.0, -1.0, 2.0)
    ]
    sources = (own_ref, pair_ref, halo_ref, far_ref)

    def blend(row):
        total = weights[0] * spread(sources[0], row)
        for w, ref in zip(weights[1:], sources[1:]):
            total = total + w * spread(ref, row)
        return total

    for level in range(levels):
        total = members_ref[0, level].astype(F32)
        for k in range(1, ens):
            total = total + members_ref[k, level].astype(F32)
        mean = total / ens
        shift = mean
        for k in range(ens):
            pert = members_ref[k, level].astype(F32) - mean
            pert_s[k * levels + level] = pert
        mean_s[level] = shift
    for j in range(ens):
        shared = blend(tri + j)
        for level in range(levels):
            mean_s[level] = mean_s[level] + pert_s[j * levels + level] * shared

    for ib in range(nb):

        def rows(step, _, ib=ib):
            i = ib * SUB + step
            start = base[ib * SUB] + step * SUB * (nb - ib)
            for kb in range(ib, nb):
                for s in range(SUB):
                    value = blend(start + SUB * (kb - ib) + s)
                    tx_s[i * ens + SUB * kb + s] = value
                    if kb > ib:
                        tx_s[(SUB * kb + s) * ens + i] = value
            return 0

        lax.fori_loop(0, SUB, rows, 0)

    wide = 4

    def body(step, _):
        k0 = step * wide
        for l0 in range(0, levels, wide):
            acc = [[mean_s[l0 + l] for l in range(wide)] for _ in range(wide)]
            for j in range(ens):
                pert = [pert_s[j * levels + l0 + l] for l in range(wide)]
                for k in range(wide):
                    t = tx_s[j * ens + k0 + k]
                    for l in range(wide):
                        acc[k][l] = acc[k][l] + t * pert[l]
            for k in range(wide):
                for l in range(wide):
                    out_ref[k0 + k, l0 + l] = acc[k][l].astype(BF16)
        return 0

    lax.fori_loop(0, ens // wide, body, 0)


def update(gz, members, own, pair, halo, far):
    ens, levels, width_x, width_y = members.shape
    vmem = pl.BlockSpec(memory_space=pltpu.VMEM)
    tile = (width_x, width_y)
    return pl.pallas_call(
        update_kernel,
        out_shape=jax.ShapeDtypeStruct(members.shape, BF16),
        in_specs=[pl.BlockSpec(memory_space=pltpu.SMEM)] + [vmem] * 5,
        out_specs=vmem,
        scratch_shapes=[
            pltpu.VMEM((ens * levels,) + tile, F32),
            pltpu.VMEM((levels,) + tile, F32),
            pltpu.VMEM((ens * ens,) + tile, F32),
        ],
        compiler_params=params(),
        name="update",
    )(gz, members, own, pair, halo, far)


def shifted(x, axis, shift):
    size = lax.axis_size(axis)
    return lax.ppermute(x, axis, [((i + shift) % size, i) for i in range(size)])


def swapped(x):
    return lax.ppermute(x, "gz", [(0, 1), (1, 0)])


def signed(index, count):
    return index if index <= count // 2 else index - count


def per_device(
    members, obs_value, obs_rinv, obs_count, stencil_cell, stencil_weight, patch_list, patch_taper
):
    ens = members.shape[0]
    slots = obs_value.shape[-1]
    size_x, size_y = lax.axis_size("gx"), lax.axis_size("gy")
    n_x, n_y = min(size_x, 5), min(size_y, 3)
    gz = lax.axis_index("gz")
    gz_arg = gz.reshape(1).astype(jnp.int32)

    lists = jnp.concatenate([patch_list.astype(F32), patch_taper], axis=-1)
    own_list = lax.dynamic_index_in_dim(lists, gz, 0, keepdims=False)
    sent_list = lax.dynamic_index_in_dim(lists, 1 - gz, 0, keepdims=False)
    turn = [(2 * i, 2 * ((i + 1) % size_x)) for i in range(size_x)]
    turn += [(2 * i + 1, 2 * ((i - 1) % size_x) + 1) for i in range(size_x)]
    halo_list = lax.ppermute(sent_list, ("gx", "gz"), turn)

    packet = observe(
        members,
        stencil_cell.reshape(-1, slots),
        stencil_weight.reshape(-1, slots),
        obs_value.reshape(1, slots),
        obs_rinv.reshape(1, slots),
        obs_count.reshape(1),
    )
    high, low = dense_tapers(gz_arg, own_list, halo_list, n_x, n_y, slots)

    along = [packet] + [shifted(packet, "gx", signed(x, n_x)) for x in range(1, n_x)]
    along = jnp.stack(along, axis=0)
    across = [along] + [shifted(along, "gy", signed(y, n_y)) for y in range(1, n_y)]
    here = jnp.stack(across, axis=1).reshape(n_x * n_y, ens + SUB, slots)
    there = swapped(here)

    gram = grams((here, there), high, low, ens)
    own = roots(gram, 0, ens)
    pair = swapped(own)
    halo = roots(gram, 1, ens)
    far = swapped(halo)
    return update(gz_arg, members, own, pair, halo, far)


def solution(mesh):
    return jax.shard_map(
        per_device,
        mesh=mesh,
        in_specs=(
            P("groups", "gz", "gx", "gy"),
            P(("groups", "gz"), "gx", "gy", None),
            P(("groups", "gz"), "gx", "gy", None),
            P(("groups", "gz"), "gx", "gy"),
            P(("groups", "gz"), "gx", "gy", None, None),
            P(("groups", "gz"), "gx", "gy", None, None),
            P(("groups", "gx"), "gy", None),
            P(("groups", "gx"), "gy", None),
        ),
        out_specs=P("groups", "gz", "gx", "gy"),
        check_vma=False,
    )
```

```python
import functools
import math

import jax
import jax.numpy as jnp
from jax import lax
from jax.experimental import pallas as pl
from jax.experimental.pallas import tpu as pltpu
from jax.sharding import PartitionSpec as P

PX = 4
F32 = jnp.float32
BF16 = jnp.bfloat16
LANES = 128
SUB = 8
VMEM_LIMIT = 40 << 20


def params():
    return pltpu.CompilerParams(vmem_limit_bytes=VMEM_LIMIT)


def micros(time):
    return pl.CostEstimate(flops=int(time * 1e9), bytes_accessed=int(time * 3e6), transcendentals=0)


def spread(ref, row):
    return ref[pl.ds(row, SUB, stride=0), :]


def block_base(ens):
    nb = ens // SUB
    base, at = [], 0
    for i in range(ens):
        base.append(at)
        at += SUB * (nb - i // SUB)
    return base, at


def observe_kernel(
    gz_ref, count_ref, members_in, cell_in, weight_in, value_in, rinv_in, ids_in, tapers_in,
    out_ref, sent_ref, own_ref,
    members_ref, cell_ref, weight_ref, value_ref, rinv_ref, ids_ref, tapers_ref, wx, pick, part, sems,
):
    ins = (cell_in, weight_in, members_in, value_in, rinv_in, ids_in, tapers_in)
    here = (cell_ref, weight_ref, members_ref, value_ref, rinv_ref, ids_ref, tapers_ref)
    copies = [pltpu.make_async_copy(src, dst, sems.at[n]) for n, (src, dst) in enumerate(zip(ins, here))]
    for copy in copies:
        copy.start()
    copies[0].wait()
    copies[1].wait()
    ens, levels, width_x, width_y = members_ref.shape
    slots = cell_ref.shape[1]
    sten = cell_ref.shape[0]
    cell = cell_ref[...]
    low = jnp.bitwise_and(cell, width_y - 1)
    high = lax.shift_right_logical(cell, width_y.bit_length() - 1)
    low0 = jnp.min(low, axis=0, keepdims=True)
    code = high * 2 + (low - low0)
    weight = weight_ref[...]
    x_iota = lax.broadcasted_iota(jnp.int32, (width_x, slots), 0)
    for level in range(levels):
        for c in range(2):
            want = (level * width_x + x_iota) * 2 + c
            total = jnp.zeros((width_x, slots), F32)
            for s in range(sten):
                total = total + jnp.where(code[s : s + 1] == want, weight[s : s + 1], 0.0)
            wx[c, level * width_x : (level + 1) * width_x, :] = total
    y_iota = lax.broadcasted_iota(jnp.int32, (width_y, slots), 0)
    pick[:, :slots] = jnp.where(y_iota == low0, 1.0, 0.0).astype(BF16)
    pick[:, slots:] = jnp.where(y_iota == low0 + 1, 1.0, 0.0).astype(BF16)
    copies[2].wait()

    def member(k, _):
        rows = members_ref[k].astype(F32).reshape(levels * width_x, width_y).astype(BF16)
        got = jnp.dot(rows, pick[...], preferred_element_type=F32)
        term = got[:, :slots] * wx[0] + got[:, slots:] * wx[1]
        total = term[:SUB]
        for q in range(1, levels * width_x // SUB):
            total = total + term[q * SUB : (q + 1) * SUB]
        for half in range(slots // LANES):
            part[half, pl.ds(pl.multiple_of(k * SUB, SUB), SUB), :] = total[:, half * LANES : (half + 1) * LANES]
        return 0

    lax.fori_loop(0, ens, member, 0, unroll=2)
    groups = []
    for kb in range(ens // SUB):
        halves = []
        for half in range(slots // LANES):
            total = part[half, pl.ds(kb * SUB * SUB, SUB, stride=SUB), :]
            for s in range(1, SUB):
                total = total + part[half, pl.ds(kb * SUB * SUB + s, SUB, stride=SUB), :]
            halves.append(total)
        groups.append(jnp.concatenate(halves, axis=1))
    total = groups[0]
    for group in groups[1:]:
        total = total + group
    mean = jnp.sum(total, axis=0, keepdims=True) / ens
    for kb in range(ens // SUB):
        out_ref[kb * SUB : (kb + 1) * SUB, :] = groups[kb] - mean
    for copy in copies[3:]:
        copy.wait()
    live = lax.broadcasted_iota(jnp.int32, (1, slots), 1) < count_ref[0]
    innovation = value_ref[...] - mean
    rinv = jnp.where(live, rinv_ref[...], 0.0)
    row = lax.broadcasted_iota(jnp.int32, (SUB, slots), 0)
    out_ref[ens : ens + SUB, :] = jnp.where(row == 0, innovation, jnp.where(row == 1, rinv, 0.0))
    sent_ref[: ens + SUB, :] = out_ref[...]
    gz = gz_ref[0]
    own_ref[...] = jnp.concatenate([ids_ref[gz].astype(F32), tapers_ref[gz]], axis=1)
    other = jnp.concatenate([ids_ref[1 - gz].astype(F32), tapers_ref[1 - gz]], axis=1)
    parts = slots // other.shape[1]
    rows = other.shape[0] // parts
    for q in range(parts):
        lanes = slice(q * other.shape[1], (q + 1) * other.shape[1])
        sent_ref[ens + SUB :, lanes] = other[q * rows : (q + 1) * rows]


def observe(gz, count, members, cell, weight, value, rinv, ids, tapers):
    ens, levels, width_x, width_y = members.shape
    sten, slots = cell.shape
    _, patches, mloc = ids.shape
    vmem = pl.BlockSpec(memory_space=pltpu.VMEM)
    smem = pl.BlockSpec(memory_space=pltpu.SMEM)
    extra = patches * 2 * mloc // slots
    return pl.pallas_call(
        observe_kernel,
        out_shape=(
            jax.ShapeDtypeStruct((ens + SUB, slots), F32),
            jax.ShapeDtypeStruct((ens + SUB + extra, slots), F32),
            jax.ShapeDtypeStruct((patches, 2 * mloc), F32),
        ),
        in_specs=[smem, smem] + [pl.BlockSpec(memory_space=pl.ANY)] * 7,
        out_specs=(vmem, vmem, vmem),
        scratch_shapes=[
            pltpu.VMEM(members.shape, members.dtype),
            pltpu.VMEM(cell.shape, cell.dtype),
            pltpu.VMEM(weight.shape, F32),
            pltpu.VMEM(value.shape, F32),
            pltpu.VMEM(rinv.shape, F32),
            pltpu.VMEM(ids.shape, ids.dtype),
            pltpu.VMEM(tapers.shape, F32),
            pltpu.VMEM((2, levels * width_x, slots), F32),
            pltpu.VMEM((width_y, 2 * slots), BF16),
            pltpu.VMEM((slots // LANES, ens * SUB, LANES), F32),
            pltpu.SemaphoreType.DMA((7,)),
        ],
        compiler_params=params(),
        cost_estimate=micros(3),
        name="observe",
    )(gz, count, members, cell, weight, value, rinv, ids, tapers)


def taper_kernel(gz_ref, list_ref, high_ref, low_ref, list_s, code_s, slot_s, taper_s, *, shift, n_x, n_y, slots, mloc):
    patches = high_ref.shape[1]
    batch = patches // SUB
    gz = gz_ref[0]
    n_buf = 2 * n_x * n_y
    lanes = SUB * mloc
    span = list_ref.shape[0]
    for n in range(patches // span):
        list_s[n * span : (n + 1) * span, :] = list_ref[:, n * 2 * mloc : (n + 1) * 2 * mloc]
    pairs = [list_s[pl.ds(q, batch, stride=SUB), :] for q in range(SUB)]
    ids = jnp.concatenate([pair[:, :mloc] for pair in pairs], axis=1).astype(jnp.int32)
    taper = jnp.concatenate([pair[:, mloc:] for pair in pairs], axis=1)
    tile = lax.shift_right_logical(ids, slots.bit_length() - 1)
    upper = (tile >= 9).astype(jnp.int32)
    tile = tile - 9 * upper
    a = (tile >= 3).astype(jnp.int32) + (tile >= 6).astype(jnp.int32)
    b = tile - 3 * a
    other = jnp.where(upper == gz, 0, 1)
    x = jnp.where(gz == 0, a - 1, 1 - a) + shift
    x = lax.rem(jnp.where(other == 0, x, -x) + 2 * n_x, n_x)
    y = lax.rem(b - 1 + n_y, n_y)
    patch = lax.shift_right_logical(lax.broadcasted_iota(jnp.int32, ids.shape, 1), mloc.bit_length() - 1)
    code_s[...] = ((other * n_x + x) * n_y + y) * SUB + patch
    slot_s[...] = jnp.bitwise_and(ids, slots - 1)
    taper_s[...] = taper

    def dense(it):
        code = code_s[pl.ds(it, 1), :]
        slot = slot_s[pl.ds(it, 1), :]
        taper = taper_s[pl.ds(it, 1), :]
        hit = lax.broadcasted_iota(jnp.int32, (n_buf * SUB, lanes), 0) == code
        coarse = taper.astype(BF16).astype(F32)
        left = jnp.concatenate(
            [jnp.where(hit, coarse, 0.0).astype(BF16), jnp.where(hit, taper - coarse, 0.0).astype(BF16)], axis=0
        )
        right = jnp.where(lax.broadcasted_iota(jnp.int32, (slots, lanes), 0) == slot, 1.0, 0.0).astype(BF16)
        both = lax.dot_general(left, right, (((1,), (1,)), ((), ())), preferred_element_type=F32)
        return both[: n_buf * SUB] + both[n_buf * SUB :]

    def body(it, _):
        first = dense(2 * it)
        second = dense(2 * it + 1)
        for n in range(n_buf):
            rows = slice(n * SUB, (n + 1) * SUB)
            block = jnp.concatenate([first[rows], second[rows]], axis=0)
            high = block.astype(BF16)
            at = pl.ds(pl.multiple_of(it * 2 * SUB, 2 * SUB), 2 * SUB)
            high_ref[n, at, :] = high
            low_ref[n, at, :] = (block - high.astype(F32)).astype(BF16)
        return 0

    lax.fori_loop(0, batch // 2, body, 0)


def dense_tapers(gz, lists, shift, patches, mloc, n_x, n_y, slots):
    vmem = pl.BlockSpec(memory_space=pltpu.VMEM)
    n_buf = 2 * n_x * n_y
    shape = jax.ShapeDtypeStruct((n_buf, patches, slots), BF16)
    batch = patches // SUB
    return pl.pallas_call(
        functools.partial(taper_kernel, shift=shift, n_x=n_x, n_y=n_y, slots=slots, mloc=mloc),
        out_shape=(shape, shape),
        in_specs=[pl.BlockSpec(memory_space=pltpu.SMEM), vmem],
        out_specs=(vmem, vmem),
        scratch_shapes=[
            pltpu.VMEM((patches, 2 * mloc), F32),
            pltpu.VMEM((batch, SUB * mloc), jnp.int32),
            pltpu.VMEM((batch, SUB * mloc), jnp.int32),
            pltpu.VMEM((batch, SUB * mloc), F32),
        ],
        compiler_params=params(),
        cost_estimate=micros(3),
        name="dense_tapers",
    )(gz, lists)


def gram_kernel(*refs, ens, n_parts, first_buf, carry):
    refs = list(refs)
    before = refs.pop(0) if carry else None
    stacks = refs[:n_parts]
    own_high, own_low, halo_high, halo_low, out_ref, z_s, zr_s = refs[n_parts:]
    nb = ens // SUB
    base, tri = block_base(ens)
    rows = tri + ens
    nt = (((1,), (1,)), ((), ()))
    n = first_buf
    for stack in stacks:
        for t in range(stack.shape[0]):
            ob = stack[t, :ens, :]
            rinv = stack[t, ens + 1 : ens + 2, :]
            zr_s[...] = ob * rinv
            wi = stack[t, ens : ens + 1, :]
            for i in range(0, ens, 2):
                ib = i // SUB
                part = jnp.concatenate(
                    [ob[kb * SUB : (kb + 1) * SUB] * zr_s[q : q + 1, :] for q in (i, i + 1) for kb in range(ib, nb)], axis=0
                )
                high = part.astype(BF16)
                z_s[base[i] : base[i] + part.shape[0], :] = high
                z_s[rows + base[i] : rows + base[i] + part.shape[0], :] = (part - high.astype(F32)).astype(BF16)
            part = zr_s[...] * wi
            high = part.astype(BF16)
            z_s[tri:rows, :] = high
            z_s[rows + tri : 2 * rows, :] = (part - high.astype(F32)).astype(BF16)
            right = jnp.concatenate([own_high[n], halo_high[n]], axis=0)
            got = lax.dot_general(z_s[...], right, nt, preferred_element_type=F32)
            right = jnp.concatenate([own_low[n], halo_low[n]], axis=0)
            more = lax.dot_general(z_s[:rows, :], right, nt, preferred_element_type=F32)
            total = got[:rows] + (got[rows:] + more)
            if n > first_buf:
                total = out_ref[...] + total
            elif carry:
                total = before[...] + total
            out_ref[...] = total
            n += 1


def grams(stacks, tapers, ens, first_buf, before=None):
    vmem = pl.BlockSpec(memory_space=pltpu.VMEM)
    _, tri = block_base(ens)
    rows = tri + ens
    _, patches, slots = tapers[0].shape
    carry = before is not None
    args = ((before,) if carry else ()) + tuple(stacks) + tuple(tapers)
    return pl.pallas_call(
        functools.partial(gram_kernel, ens=ens, n_parts=len(stacks), first_buf=first_buf, carry=carry),
        out_shape=jax.ShapeDtypeStruct((rows, 2 * patches), F32),
        in_specs=[vmem] * len(args),
        out_specs=vmem,
        scratch_shapes=[pltpu.VMEM((2 * rows, slots), BF16), pltpu.VMEM((ens, slots), F32)],
        compiler_params=params(),
        cost_estimate=micros(2),
        name="grams",
    )(*args)


def product(ens, a, b, dests, epilogue):
    nb = ens // SUB
    for ib in range(nb):
        n = nb - ib
        rows = 4 if n > 2 else 8

        def body(step, _, ib=ib, n=n, rows=rows):
            i0 = ib * SUB + step * rows
            acc = [[None] * n for _ in range(rows)]
            for j in range(ens):
                right = [b[j * ens + SUB * kb : j * ens + SUB * (kb + 1), :] for kb in range(ib, nb)]
                for ii in range(rows):
                    left = spread(a, (i0 + ii) * ens + j)
                    for q in range(n):
                        term = left * right[q]
                        acc[ii][q] = term if j == 0 else acc[ii][q] + term
            for ii in range(rows):
                for q in range(n):
                    kb = ib + q
                    eye = None
                    if q == 0:
                        eye = lax.broadcasted_iota(jnp.int32, (SUB, LANES), 0) == step * rows + ii
                    outs = epilogue(acc[ii][q], pl.ds((i0 + ii) * ens + SUB * kb, SUB), eye)
                    for dest, value in zip(dests, outs):
                        dest[pl.ds((i0 + ii) * ens + SUB * kb, SUB), :] = value
                        if kb > ib:
                            dest[pl.ds(SUB * kb * ens + i0 + ii, SUB, stride=ens), :] = value
            return 0

        lax.fori_loop(0, SUB // rows, body, 0)


def root_kernel(gram_ref, out_ref, s_a, s_b, s_c, s_d, vec, *, ens):
    nb = ens // SUB
    base, tri = block_base(ens)
    diag = gram_ref[0:1, :]
    for i in range(1, ens):
        at = base[i] + i % SUB
        diag = diag + gram_ref[at : at + 1, :]
    half = 0.5 * (diag + (ens - 1.0) * ens)
    scale = jnp.broadcast_to(1.0 / half, (SUB, LANES))
    iota = lax.broadcasted_iota(jnp.int32, (SUB, LANES), 0)
    for i in range(ens):
        for kb in range(i // SUB, nb):
            at = base[i] + SUB * (kb - i // SUB)
            value = gram_ref[at : at + SUB, :]
            if kb == i // SUB:
                value = jnp.where(iota == i % SUB, value + (ens - 1.0), value)
            value = value * scale
            s_a[i * ens + SUB * kb : i * ens + SUB * (kb + 1), :] = value
            if kb > i // SUB:
                s_a[pl.ds(SUB * kb * ens + i, SUB, stride=ens), :] = value

    def plain(acc, at, eye):
        return (acc,)

    def quadratic(lin):
        def epilogue(acc, at, eye):
            rest = 0.0625 * acc - 0.5625 * lin[at, :]
            if eye is not None:
                rest = jnp.where(eye, rest + 1.6875, rest)
            return (acc, rest)

        return epilogue

    def quartic(lin):
        def epilogue(acc, at, eye):
            rest = acc - 2.4375 * lin[at, :]
            if eye is not None:
                rest = jnp.where(eye, rest + 2.25, rest)
            return (rest,)

        return epilogue

    product(ens, s_a, s_a, (s_b, s_c), quadratic(s_a))
    product(ens, s_b, s_c, (s_d,), quartic(s_a))
    product(ens, s_d, s_d, (s_b,), plain)
    product(ens, s_a, s_b, (s_c,), plain)
    product(ens, s_c, s_c, (s_a, s_b), quadratic(s_c))
    product(ens, s_a, s_b, (vec.at[pl.ds(0, ens * ens)],), quartic(s_c))
    product(ens, s_d, vec.at[pl.ds(0, ens * ens)], (s_a,), plain)

    right = ens * ens
    vec[right : right + ens, :] = gram_ref[tri : tri + ens, :]

    def apply(source):
        sums = [None] * nb
        for i in range(ens):
            left = spread(vec, source + i)
            for kb in range(nb):
                term = left * s_a[i * ens + SUB * kb : i * ens + SUB * (kb + 1), :]
                sums[kb] = term if i == 0 else sums[kb] + term
        return sums

    inner = apply(right)
    for kb in range(nb):
        vec[right + ens + SUB * kb : right + ens + SUB * (kb + 1), :] = inner[kb]
    outer = apply(right + ens)
    for kb in range(nb):
        out_ref[tri + SUB * kb : tri + SUB * (kb + 1), :] = outer[kb] * scale
    factor = jnp.broadcast_to(math.sqrt(ens - 1.0) / jnp.sqrt(half), (SUB, LANES))
    for i in range(ens):
        for kb in range(i // SUB, nb):
            at = base[i] + SUB * (kb - i // SUB)
            out_ref[at : at + SUB, :] = s_a[i * ens + SUB * kb : i * ens + SUB * (kb + 1), :] * factor


def roots(gram, row, ens):
    rows = gram.shape[0]
    square = pltpu.VMEM((ens * ens, LANES), F32)
    return pl.pallas_call(
        functools.partial(root_kernel, ens=ens),
        out_shape=jax.ShapeDtypeStruct((rows, LANES), F32),
        grid=(1,),
        in_specs=[pl.BlockSpec((rows, LANES), lambda g: (0, row))],
        out_specs=pl.BlockSpec((rows, LANES), lambda g: (0, 0)),
        scratch_shapes=[square] * 4 + [pltpu.VMEM((ens * ens + 2 * ens, LANES), F32)],
        compiler_params=params(),
        cost_estimate=micros(7),
        name="roots",
    )(gram)


def update_kernel(gz_ref, members_ref, own_ref, pair_ref, halo_ref, far_ref, out_ref, pert_s, mean_s, tx_s):
    ens, levels, width_x, width_y = members_ref.shape
    nb = ens // SUB
    base, tri = block_base(ens)
    column = lax.broadcasted_iota(jnp.int32, (width_x, width_y), 0)
    column = jnp.where(gz_ref[0] == 0, column, width_x - 1 - column).astype(F32)
    place = (column + 0.5) / PX - 0.5
    weights = [
        jnp.maximum(0.0, 1.0 - jnp.abs(place - centre)) for centre in (0.0, 1.0, -1.0, 2.0)
    ]
    sources = (own_ref, pair_ref, halo_ref, far_ref)

    def blend(row):
        total = weights[0] * spread(sources[0], row)
        for w, ref in zip(weights[1:], sources[1:]):
            total = total + w * spread(ref, row)
        return total

    for level in range(levels):
        total = members_ref[0, level].astype(F32)
        for k in range(1, ens):
            total = total + members_ref[k, level].astype(F32)
        mean = total / ens
        shift = mean
        for k in range(ens):
            pert = members_ref[k, level].astype(F32) - mean
            pert_s[k * levels + level] = pert
        mean_s[level] = shift
    for j in range(ens):
        shared = blend(tri + j)
        for level in range(levels):
            mean_s[level] = mean_s[level] + pert_s[j * levels + level] * shared

    for ib in range(nb):

        def rows(step, _, ib=ib):
            i = ib * SUB + step
            start = base[ib * SUB] + step * SUB * (nb - ib)
            for kb in range(ib, nb):
                for s in range(SUB):
                    value = blend(start + SUB * (kb - ib) + s)
                    tx_s[i * ens + SUB * kb + s] = value
                    if kb > ib:
                        tx_s[(SUB * kb + s) * ens + i] = value
            return 0

        lax.fori_loop(0, SUB, rows, 0)

    wide = 4

    def body(step, _):
        k0 = step * wide
        for l0 in range(0, levels, wide):
            acc = [[mean_s[l0 + l] for l in range(wide)] for _ in range(wide)]
            for j in range(ens):
                pert = [pert_s[j * levels + l0 + l] for l in range(wide)]
                for k in range(wide):
                    t = tx_s[j * ens + k0 + k]
                    for l in range(wide):
                        acc[k][l] = acc[k][l] + t * pert[l]
            for k in range(wide):
                for l in range(wide):
                    out_ref[k0 + k, l0 + l] = acc[k][l].astype(BF16)
        return 0

    lax.fori_loop(0, ens // wide, body, 0)


def update(gz, members, own, pair, halo, far):
    ens, levels, width_x, width_y = members.shape
    vmem = pl.BlockSpec(memory_space=pltpu.VMEM)
    tile = (width_x, width_y)
    return pl.pallas_call(
        update_kernel,
        out_shape=jax.ShapeDtypeStruct(members.shape, BF16),
        in_specs=[pl.BlockSpec(memory_space=pltpu.SMEM)] + [vmem] * 5,
        out_specs=vmem,
        scratch_shapes=[
            pltpu.VMEM((ens * levels,) + tile, F32),
            pltpu.VMEM((levels,) + tile, F32),
            pltpu.VMEM((ens * ens,) + tile, F32),
        ],
        compiler_params=params(),
        cost_estimate=micros(4),
        name="update",
    )(gz, members, own, pair, halo, far)


def shifted(x, axis, shift):
    size = lax.axis_size(axis)
    return lax.ppermute(x, axis, [((i + shift) % size, i) for i in range(size)])


def turned(x, shift):
    size = lax.axis_size("gx")
    pairs = [(2 * ((i + shift) % size), 2 * i) for i in range(size)]
    pairs += [(2 * ((i - shift) % size) + 1, 2 * i + 1) for i in range(size)]
    return lax.ppermute(x, ("gx", "gz"), pairs)


def swapped(x):
    return lax.ppermute(x, "gz", [(0, 1), (1, 0)])


def signed(index, count):
    return index if index <= count // 2 else index - count


def after(x, *others):
    return lax.optimization_barrier((x,) + others)[0]


def per_device(
    members, obs_value, obs_rinv, obs_count, stencil_cell, stencil_weight, patch_list, patch_taper
):
    ens = members.shape[0]
    slots = obs_value.shape[-1]
    _, patches, mloc = patch_list.shape
    size_x, size_y = lax.axis_size("gx"), lax.axis_size("gy")
    n_x, n_y = min(size_x, 5), min(size_y, 3)
    gz = lax.axis_index("gz").reshape(1).astype(jnp.int32)
    packet, sent, own_list = observe(
        gz,
        obs_count.reshape(1),
        members,
        stencil_cell.reshape(-1, slots),
        stencil_weight.reshape(-1, slots),
        obs_value.reshape(1, slots),
        obs_rinv.reshape(1, slots),
        patch_list,
        patch_taper,
    )
    rows = ens + SUB
    along = {x: turned(packet, signed(x, n_x)) for x in range(1, n_x - 1)}
    halo = turned(sent, -1)
    along[n_x - 1] = halo[:rows]
    along[0] = packet
    halo_list = halo[rows:]
    own_tapers = dense_tapers(gz, own_list, 0, patches, mloc, n_x, n_y, slots)
    along = jnp.stack([along[x] for x in range(n_x)], axis=0)
    along = after(along, *own_tapers)
    across = [along] + [shifted(along, "gy", signed(y, n_y)) for y in range(1, n_y)]
    halo_tapers = dense_tapers(gz, halo_list, -1, patches, mloc, n_x, n_y, slots)
    here = jnp.stack(across, axis=1).reshape(n_x * n_y, rows, slots)
    here = after(here, *halo_tapers)
    there = swapped(here)
    tapers = own_tapers + halo_tapers
    gram = grams((here,), tapers, ens, 0)
    gram = grams((there,), tapers, ens, n_x * n_y, gram)
    own = roots(gram, 0, ens)
    pair = swapped(own)
    halo = roots(after(gram, own), 1, ens)
    far = swapped(halo)
    return update(gz, members, own, pair, halo, far)


def solution(mesh):
    return jax.shard_map(
        per_device,
        mesh=mesh,
        in_specs=(
            P("groups", "gz", "gx", "gy"),
            P(("groups", "gz"), "gx", "gy", None),
            P(("groups", "gz"), "gx", "gy", None),
            P(("groups", "gz"), "gx", "gy"),
            P(("groups", "gz"), "gx", "gy", None, None),
            P(("groups", "gz"), "gx", "gy", None, None),
            P(("groups", "gx"), "gy", None),
            P(("groups", "gx"), "gy", None),
        ),
        out_specs=P("groups", "gz", "gx", "gy"),
        check_vma=False,
    )
```

```python
import functools
import math

import jax
import jax.numpy as jnp
from jax import lax
from jax.experimental import pallas as pl
from jax.experimental.pallas import tpu as pltpu
from jax.sharding import PartitionSpec as P

PX = 4
F32 = jnp.float32
BF16 = jnp.bfloat16
LANES = 128
SUB = 8
VMEM_LIMIT = 40 << 20
WHOLE_VMEM = (64 << 20) - (256 << 10)


def params(limit=VMEM_LIMIT):
    return pltpu.CompilerParams(vmem_limit_bytes=limit)


def micros(time):
    return pl.CostEstimate(flops=int(time * 1e9), bytes_accessed=int(time * 3e6), transcendentals=0)


def spread(ref, row):
    return ref[pl.ds(row, SUB, stride=0), :]


def block_base(ens):
    nb = ens // SUB
    base, at = [], 0
    for i in range(ens):
        base.append(at)
        at += SUB * (nb - i // SUB)
    return base, at


def observe_kernel(
    gz_ref, count_ref, members_in, cell_in, weight_in, value_in, rinv_in, ids_in, tapers_in,
    out_ref, sent_ref, own_ref,
    members_ref, cell_ref, weight_ref, value_ref, rinv_ref, ids_ref, tapers_ref, wx, pick, part, sems,
):
    ins = (cell_in, weight_in, members_in, value_in, rinv_in, ids_in, tapers_in)
    here = (cell_ref, weight_ref, members_ref, value_ref, rinv_ref, ids_ref, tapers_ref)
    copies = [pltpu.make_async_copy(src, dst, sems.at[n]) for n, (src, dst) in enumerate(zip(ins, here))]
    for copy in copies:
        copy.start()
    copies[0].wait()
    copies[1].wait()
    ens, levels, width_x, width_y = members_ref.shape
    slots = cell_ref.shape[1]
    sten = cell_ref.shape[0]
    cell = cell_ref[...]
    low = jnp.bitwise_and(cell, width_y - 1)
    high = lax.shift_right_logical(cell, width_y.bit_length() - 1)
    low0 = jnp.min(low, axis=0, keepdims=True)
    code = high * 2 + (low - low0)
    weight = weight_ref[...]
    x_iota = lax.broadcasted_iota(jnp.int32, (width_x, slots), 0)
    for level in range(levels):
        for c in range(2):
            want = (level * width_x + x_iota) * 2 + c
            total = jnp.zeros((width_x, slots), F32)
            for s in range(sten):
                total = total + jnp.where(code[s : s + 1] == want, weight[s : s + 1], 0.0)
            wx[c, level * width_x : (level + 1) * width_x, :] = total
    y_iota = lax.broadcasted_iota(jnp.int32, (width_y, slots), 0)
    pick[:, :slots] = jnp.where(y_iota == low0, 1.0, 0.0).astype(BF16)
    pick[:, slots:] = jnp.where(y_iota == low0 + 1, 1.0, 0.0).astype(BF16)
    copies[2].wait()

    def member(k, _):
        rows = members_ref[k].astype(F32).reshape(levels * width_x, width_y).astype(BF16)
        got = jnp.dot(rows, pick[...], preferred_element_type=F32)
        term = got[:, :slots] * wx[0] + got[:, slots:] * wx[1]
        total = term[:SUB]
        for q in range(1, levels * width_x // SUB):
            total = total + term[q * SUB : (q + 1) * SUB]
        for half in range(slots // LANES):
            part[half, pl.ds(pl.multiple_of(k * SUB, SUB), SUB), :] = total[:, half * LANES : (half + 1) * LANES]
        return 0

    lax.fori_loop(0, ens, member, 0, unroll=8)
    groups = []
    for kb in range(ens // SUB):
        halves = []
        for half in range(slots // LANES):
            total = part[half, pl.ds(kb * SUB * SUB, SUB, stride=SUB), :]
            for s in range(1, SUB):
                total = total + part[half, pl.ds(kb * SUB * SUB + s, SUB, stride=SUB), :]
            halves.append(total)
        groups.append(jnp.concatenate(halves, axis=1))
    total = groups[0]
    for group in groups[1:]:
        total = total + group
    mean = jnp.sum(total, axis=0, keepdims=True) / ens
    for kb in range(ens // SUB):
        out_ref[kb * SUB : (kb + 1) * SUB, :] = groups[kb] - mean
    for copy in copies[3:]:
        copy.wait()
    live = lax.broadcasted_iota(jnp.int32, (1, slots), 1) < count_ref[0]
    innovation = value_ref[...] - mean
    rinv = jnp.where(live, rinv_ref[...], 0.0)
    row = lax.broadcasted_iota(jnp.int32, (SUB, slots), 0)
    out_ref[ens : ens + SUB, :] = jnp.where(row == 0, innovation, jnp.where(row == 1, rinv, 0.0))
    gz = gz_ref[0]
    own_ref[...] = jnp.concatenate([ids_ref[gz].astype(F32), tapers_ref[gz]], axis=0).T
    sent_ref[...] = jnp.concatenate([ids_ref[1 - gz].astype(F32), tapers_ref[1 - gz]], axis=0).T


def observe(gz, count, members, cell, weight, value, rinv, ids, tapers):
    ens, levels, width_x, width_y = members.shape
    sten, slots = cell.shape
    _, mloc, patches = ids.shape
    vmem = pl.BlockSpec(memory_space=pltpu.VMEM)
    smem = pl.BlockSpec(memory_space=pltpu.SMEM)
    return pl.pallas_call(
        observe_kernel,
        out_shape=(
            jax.ShapeDtypeStruct((ens + SUB, slots), F32),
            jax.ShapeDtypeStruct((patches, 2 * mloc), F32),
            jax.ShapeDtypeStruct((patches, 2 * mloc), F32),
        ),
        in_specs=[smem, smem] + [pl.BlockSpec(memory_space=pltpu.HBM)] * 7,
        out_specs=(vmem, vmem, vmem),
        scratch_shapes=[
            pltpu.VMEM(members.shape, members.dtype),
            pltpu.VMEM(cell.shape, cell.dtype),
            pltpu.VMEM(weight.shape, F32),
            pltpu.VMEM(value.shape, F32),
            pltpu.VMEM(rinv.shape, F32),
            pltpu.VMEM(ids.shape, ids.dtype),
            pltpu.VMEM(tapers.shape, F32),
            pltpu.VMEM((2, levels * width_x, slots), F32),
            pltpu.VMEM((width_y, 2 * slots), BF16),
            pltpu.VMEM((slots // LANES, ens * SUB, LANES), F32),
            pltpu.SemaphoreType.DMA((7,)),
        ],
        compiler_params=params(WHOLE_VMEM),
        cost_estimate=micros(3),
        name="observe",
    )(gz, count, members, cell, weight, value, rinv, ids, tapers)


def taper_kernel(gz_ref, list_ref, high_ref, low_ref, code_s, slot_s, taper_s, *, shift, n_x, n_y, slots, mloc):
    patches = high_ref.shape[1]
    batch = patches // SUB
    gz = gz_ref[0]
    n_buf = 2 * n_x * n_y
    lanes = SUB * mloc
    pairs = [list_ref[pl.ds(q, batch, stride=SUB), :] for q in range(SUB)]
    ids = jnp.concatenate([pair[:, :mloc] for pair in pairs], axis=1).astype(jnp.int32)
    taper = jnp.concatenate([pair[:, mloc:] for pair in pairs], axis=1)
    tile = lax.shift_right_logical(ids, slots.bit_length() - 1)
    upper = (tile >= 9).astype(jnp.int32)
    tile = tile - 9 * upper
    a = (tile >= 3).astype(jnp.int32) + (tile >= 6).astype(jnp.int32)
    b = tile - 3 * a
    other = jnp.where(upper == gz, 0, 1)
    x = jnp.where(gz == 0, a - 1, 1 - a) + shift
    x = lax.rem(jnp.where(other == 0, x, -x) + 2 * n_x, n_x)
    y = lax.rem(b - 1 + n_y, n_y)
    patch = lax.shift_right_logical(lax.broadcasted_iota(jnp.int32, ids.shape, 1), mloc.bit_length() - 1)
    code_s[...] = (((other * n_y + y) * n_x + x) * SUB + patch).astype(F32)
    slot_s[...] = jnp.bitwise_and(ids, slots - 1).astype(F32)
    taper_s[...] = taper
    code_iota = lax.broadcasted_iota(jnp.int32, (n_buf * SUB, lanes), 0).astype(F32).astype(BF16)
    slot_iota = lax.broadcasted_iota(jnp.int32, (slots, lanes), 0).astype(F32).astype(BF16)
    zero, one = jnp.zeros((), BF16), jnp.ones((), BF16)

    def dense(it):
        code = code_s[pl.ds(it, 1), :].astype(BF16)
        slot = slot_s[pl.ds(it, 1), :].astype(BF16)
        taper = taper_s[pl.ds(it, 1), :]
        coarse = taper.astype(BF16)
        fine = (taper - coarse.astype(F32)).astype(BF16)
        hit = code_iota == code
        left = jnp.concatenate([jnp.where(hit, coarse, zero), jnp.where(hit, fine, zero)], axis=0)
        right = jnp.where(slot_iota == slot, one, zero)
        both = lax.dot_general(left, right, (((1,), (1,)), ((), ())), preferred_element_type=F32)
        return both[: n_buf * SUB] + both[n_buf * SUB :]

    def body(it, _):
        first = dense(2 * it)
        second = dense(2 * it + 1)
        for n in range(n_buf):
            rows = slice(n * SUB, (n + 1) * SUB)
            block = jnp.concatenate([first[rows], second[rows]], axis=0)
            high = block.astype(BF16)
            at = pl.ds(pl.multiple_of(it * 2 * SUB, 2 * SUB), 2 * SUB)
            high_ref[n, at, :] = high
            low_ref[n, at, :] = (block - high.astype(F32)).astype(BF16)
        return 0

    lax.fori_loop(0, batch // 2, body, 0, unroll=True)


def dense_tapers(gz, lists, shift, patches, mloc, n_x, n_y, slots):
    vmem = pl.BlockSpec(memory_space=pltpu.VMEM)
    n_buf = 2 * n_x * n_y
    shape = jax.ShapeDtypeStruct((n_buf, patches, slots), BF16)
    batch = patches // SUB
    return pl.pallas_call(
        functools.partial(taper_kernel, shift=shift, n_x=n_x, n_y=n_y, slots=slots, mloc=mloc),
        out_shape=(shape, shape),
        in_specs=[pl.BlockSpec(memory_space=pltpu.SMEM), vmem],
        out_specs=(vmem, vmem),
        scratch_shapes=[
            pltpu.VMEM((batch, SUB * mloc), F32),
            pltpu.VMEM((batch, SUB * mloc), F32),
            pltpu.VMEM((batch, SUB * mloc), F32),
        ],
        compiler_params=params(),
        cost_estimate=micros(3),
        name="dense_tapers",
    )(gz, lists)


def gram_kernel(*refs, ens, bufs, carry):
    refs = list(refs)
    before = refs.pop(0) if carry else None
    stack, own_high, own_low, halo_high, halo_low, out_ref, z_s, zr_s = refs
    nb = ens // SUB
    base, tri = block_base(ens)
    rows = tri + ens
    nt = (((1,), (1,)), ((), ()))
    for t, n in enumerate(bufs):
        ob = stack[t, :ens, :]
        rinv = stack[t, ens + 1 : ens + 2, :]
        zr_s[...] = ob * rinv
        wi = stack[t, ens : ens + 1, :]
        for i in range(0, ens, 2):
            ib = i // SUB
            part = jnp.concatenate(
                [ob[kb * SUB : (kb + 1) * SUB] * zr_s[q : q + 1, :] for q in (i, i + 1) for kb in range(ib, nb)], axis=0
            )
            high = part.astype(BF16)
            z_s[base[i] : base[i] + part.shape[0], :] = high
            z_s[rows + base[i] : rows + base[i] + part.shape[0], :] = (part - high.astype(F32)).astype(BF16)
        part = zr_s[...] * wi
        high = part.astype(BF16)
        z_s[tri:rows, :] = high
        z_s[rows + tri : 2 * rows, :] = (part - high.astype(F32)).astype(BF16)
        right = jnp.concatenate([own_high[n], halo_high[n]], axis=0)
        got = lax.dot_general(z_s[...], right, nt, preferred_element_type=F32)
        right = jnp.concatenate([own_low[n], halo_low[n]], axis=0)
        more = lax.dot_general(z_s[:rows, :], right, nt, preferred_element_type=F32)
        total = got[:rows] + (got[rows:] + more)
        if t > 0:
            total = out_ref[...] + total
        elif carry:
            total = before[...] + total
        out_ref[...] = total


def grams(stack, tapers, ens, bufs, before=None):
    vmem = pl.BlockSpec(memory_space=pltpu.VMEM)
    _, tri = block_base(ens)
    rows = tri + ens
    _, patches, slots = tapers[0].shape
    carry = before is not None
    args = ((before,) if carry else ()) + (stack,) + tuple(tapers)
    return pl.pallas_call(
        functools.partial(gram_kernel, ens=ens, bufs=tuple(bufs), carry=carry),
        out_shape=jax.ShapeDtypeStruct((rows, 2 * patches), F32),
        in_specs=[vmem] * len(args),
        out_specs=vmem,
        scratch_shapes=[pltpu.VMEM((2 * rows, slots), BF16), pltpu.VMEM((ens, slots), F32)],
        compiler_params=params(),
        cost_estimate=micros(2),
        name="grams",
    )(*args)


def product(ens, a, b, dests, epilogue):
    nb = ens // SUB
    for ib in range(nb):
        n = nb - ib
        rows = 4 if n > 2 else 8

        def body(step, _, ib=ib, n=n, rows=rows):
            i0 = ib * SUB + step * rows
            acc = [[None] * n for _ in range(rows)]
            for j in range(ens):
                right = [b[j * ens + SUB * kb : j * ens + SUB * (kb + 1), :] for kb in range(ib, nb)]
                for ii in range(rows):
                    left = spread(a, (i0 + ii) * ens + j)
                    for q in range(n):
                        term = left * right[q]
                        acc[ii][q] = term if j == 0 else acc[ii][q] + term
            for ii in range(rows):
                for q in range(n):
                    kb = ib + q
                    eye = None
                    if q == 0:
                        eye = lax.broadcasted_iota(jnp.int32, (SUB, LANES), 0) == step * rows + ii
                    outs = epilogue(acc[ii][q], pl.ds((i0 + ii) * ens + SUB * kb, SUB), eye)
                    for dest, value in zip(dests, outs):
                        dest[pl.ds((i0 + ii) * ens + SUB * kb, SUB), :] = value
                        if kb > ib:
                            dest[pl.ds(SUB * kb * ens + i0 + ii, SUB, stride=ens), :] = value
            return 0

        lax.fori_loop(0, SUB // rows, body, 0)


def root_kernel(gram_ref, out_ref, s_a, s_b, s_c, s_d, vec, *, ens):
    nb = ens // SUB
    base, tri = block_base(ens)
    diag = gram_ref[0:1, :]
    for i in range(1, ens):
        at = base[i] + i % SUB
        diag = diag + gram_ref[at : at + 1, :]
    half = 0.5 * (diag + (ens - 1.0) * ens)
    scale = jnp.broadcast_to(1.0 / half, (SUB, LANES))
    iota = lax.broadcasted_iota(jnp.int32, (SUB, LANES), 0)
    for i in range(ens):
        for kb in range(i // SUB, nb):
            at = base[i] + SUB * (kb - i // SUB)
            value = gram_ref[at : at + SUB, :]
            if kb == i // SUB:
                value = jnp.where(iota == i % SUB, value + (ens - 1.0), value)
            value = value * scale
            s_a[i * ens + SUB * kb : i * ens + SUB * (kb + 1), :] = value
            if kb > i // SUB:
                s_a[pl.ds(SUB * kb * ens + i, SUB, stride=ens), :] = value

    def plain(acc, at, eye):
        return (acc,)

    def quadratic(lin):
        def epilogue(acc, at, eye):
            rest = 0.0625 * acc - 0.5625 * lin[at, :]
            if eye is not None:
                rest = jnp.where(eye, rest + 1.6875, rest)
            return (acc, rest)

        return epilogue

    def quartic(lin):
        def epilogue(acc, at, eye):
            rest = acc - 2.4375 * lin[at, :]
            if eye is not None:
                rest = jnp.where(eye, rest + 2.25, rest)
            return (rest,)

        return epilogue

    product(ens, s_a, s_a, (s_b, s_c), quadratic(s_a))
    product(ens, s_b, s_c, (s_d,), quartic(s_a))
    product(ens, s_d, s_d, (s_b,), plain)
    product(ens, s_a, s_b, (s_c,), plain)
    product(ens, s_c, s_c, (s_a, s_b), quadratic(s_c))
    product(ens, s_a, s_b, (vec.at[pl.ds(0, ens * ens)],), quartic(s_c))
    product(ens, s_d, vec.at[pl.ds(0, ens * ens)], (s_a,), plain)

    right = ens * ens
    vec[right : right + ens, :] = gram_ref[tri : tri + ens, :]

    def apply(source):
        sums = [None] * nb
        for i in range(ens):
            left = spread(vec, source + i)
            for kb in range(nb):
                term = left * s_a[i * ens + SUB * kb : i * ens + SUB * (kb + 1), :]
                sums[kb] = term if i == 0 else sums[kb] + term
        return sums

    inner = apply(right)
    for kb in range(nb):
        vec[right + ens + SUB * kb : right + ens + SUB * (kb + 1), :] = inner[kb]
    outer = apply(right + ens)
    for kb in range(nb):
        vec[right + SUB * kb : right + SUB * (kb + 1), :] = outer[kb] * scale
    factor = jnp.broadcast_to(math.sqrt(ens - 1.0) / jnp.sqrt(half), (SUB, LANES))
    for j in range(ens):
        weight = spread(vec, right + j)
        for kb in range(nb):
            at = slice(j * ens + SUB * kb, j * ens + SUB * (kb + 1))
            out_ref[at, :] = weight + s_a[at, :] * factor


def roots(gram, row, ens):
    rows = gram.shape[0]
    square = pltpu.VMEM((ens * ens, LANES), F32)
    return pl.pallas_call(
        functools.partial(root_kernel, ens=ens),
        out_shape=jax.ShapeDtypeStruct((ens * ens, LANES), F32),
        grid=(1,),
        in_specs=[pl.BlockSpec((rows, LANES), lambda g: (0, row))],
        out_specs=pl.BlockSpec((ens * ens, LANES), lambda g: (0, 0)),
        scratch_shapes=[square] * 4 + [pltpu.VMEM((ens * ens + 2 * ens, LANES), F32)],
        compiler_params=params(),
        cost_estimate=micros(7),
        name="roots",
    )(gram)


def center_kernel(members_ref, pert_ref, mean_ref):
    ens, levels, width_x, _ = members_ref.shape
    for level in range(levels):
        total = members_ref[0, level].astype(F32)
        for k in range(1, ens):
            total = total + members_ref[k, level].astype(F32)
        mean = total / ens
        mean_ref[level * width_x : (level + 1) * width_x, :] = mean
        for k in range(ens):
            at = (k * levels + level) * width_x
            pert_ref[at : at + width_x, :] = members_ref[k, level].astype(F32) - mean


def center(members):
    ens, levels, width_x, width_y = members.shape
    vmem = pl.BlockSpec(memory_space=pltpu.VMEM)
    cells = levels * width_x
    return pl.pallas_call(
        center_kernel,
        out_shape=(
            jax.ShapeDtypeStruct((ens * cells, width_y), F32),
            jax.ShapeDtypeStruct((cells, width_y), F32),
        ),
        in_specs=[vmem],
        out_specs=(vmem, vmem),
        compiler_params=params(),
        cost_estimate=micros(1),
        name="center",
    )(members)


def columns(gz, pert_ref, mean_ref, dest, main_ref, beside_ref, first, ens, levels, width_x):
    nb = ens // SUB
    near = first % PX

    def body(step, _):
        place = jnp.abs((near + step + 0.5) / PX - 0.5)
        turned_x = first + step
        x = jnp.where(gz == 0, turned_x, width_x - 1 - turned_x)
        w_main = jnp.broadcast_to(1.0 - place, (SUB, LANES))
        w_beside = jnp.broadcast_to(place, (SUB, LANES))
        acc = [[spread(mean_ref, level * width_x + x)] * nb for level in range(levels)]
        for j in range(ens):
            blend = []
            for kb in range(nb):
                at = slice(j * ens + SUB * kb, j * ens + SUB * (kb + 1))
                blend.append(w_main * main_ref[at, :] + w_beside * beside_ref[at, :])
            for level in range(levels):
                pert = spread(pert_ref, (j * levels + level) * width_x + x)
                for kb in range(nb):
                    acc[level][kb] = acc[level][kb] + pert * blend[kb]
        for level in range(levels):
            for kb in range(nb):
                at = (SUB * kb * levels + level) * width_x + x
                dest[pl.ds(at, SUB, stride=levels * width_x), :] = acc[level][kb]
        return 0

    lax.fori_loop(0, PX // 2, body, 0)


def inner_kernel(gz_ref, pert_ref, mean_ref, own_ref, pair_ref, halo_ref, part_ref, *, ens, levels, width_x):
    gz = gz_ref[0]
    sizes = (ens, levels, width_x)
    columns(gz, pert_ref, mean_ref, part_ref, own_ref, halo_ref, 0, *sizes)
    columns(gz, pert_ref, mean_ref, part_ref, own_ref, pair_ref, PX // 2, *sizes)
    columns(gz, pert_ref, mean_ref, part_ref, pair_ref, own_ref, PX, *sizes)


def outer_kernel(gz_ref, pert_ref, mean_ref, pair_ref, far_ref, part_ref, out_ref, rest_s):
    ens, levels, width_x, width_y = out_ref.shape
    gz = gz_ref[0]
    first = 3 * PX // 2
    columns(gz, pert_ref, mean_ref, rest_s, pair_ref, far_ref, first, ens, levels, width_x)
    x = lax.broadcasted_iota(jnp.int32, (width_x, width_y), 0)
    inside = jnp.where(gz == 0, x, width_x - 1 - x) < first
    for k in range(ens):
        for level in range(levels):
            at = slice((k * levels + level) * width_x, (k * levels + level + 1) * width_x)
            out_ref[k, level] = jnp.where(inside, part_ref[at, :], rest_s[at, :]).astype(BF16)


def update(gz, shape, centred, own, pair, halo, far):
    ens, levels, width_x, width_y = shape
    pert, mean = centred
    vmem = pl.BlockSpec(memory_space=pltpu.VMEM)
    smem = pl.BlockSpec(memory_space=pltpu.SMEM)
    part = pl.pallas_call(
        functools.partial(inner_kernel, ens=ens, levels=levels, width_x=width_x),
        out_shape=jax.ShapeDtypeStruct(pert.shape, F32),
        in_specs=[smem] + [vmem] * 5,
        out_specs=vmem,
        compiler_params=params(),
        cost_estimate=micros(3),
        name="inner",
    )(gz, pert, mean, own, pair, halo)
    return pl.pallas_call(
        outer_kernel,
        out_shape=jax.ShapeDtypeStruct(shape, BF16),
        in_specs=[smem] + [vmem] * 5,
        out_specs=vmem,
        scratch_shapes=[pltpu.VMEM(pert.shape, F32)],
        compiler_params=params(),
        cost_estimate=micros(1),
        name="outer",
    )(gz, pert, mean, pair, far, part)


def shifted(x, axis, shift):
    size = lax.axis_size(axis)
    return lax.ppermute(x, axis, [((i + shift) % size, i) for i in range(size)])


def turned(x, shift):
    size = lax.axis_size("gx")
    pairs = [(2 * ((i + shift) % size), 2 * i) for i in range(size)]
    pairs += [(2 * ((i - shift) % size) + 1, 2 * i + 1) for i in range(size)]
    return lax.ppermute(x, ("gx", "gz"), pairs)


def swapped(x):
    return lax.ppermute(x, "gz", [(0, 1), (1, 0)])


def signed(index, count):
    return index if index <= count // 2 else index - count


def after(x, *others):
    return lax.optimization_barrier((x,) + others)[0]


def per_device(
    members, obs_value, obs_rinv, obs_count, stencil_cell, stencil_weight, patch_list, patch_taper
):
    ens = members.shape[0]
    slots = obs_value.shape[-1]
    _, patches, mloc = patch_list.shape
    size_x, size_y = lax.axis_size("gx"), lax.axis_size("gy")
    n_x, n_y = min(size_x, 5), min(size_y, 3)
    gz = lax.axis_index("gz").reshape(1).astype(jnp.int32)
    packet, sent, own_list = observe(
        gz,
        obs_count.reshape(1),
        members,
        stencil_cell.reshape(-1, slots),
        stencil_weight.reshape(-1, slots),
        obs_value.reshape(1, slots),
        obs_rinv.reshape(1, slots),
        jnp.swapaxes(patch_list, 1, 2),
        jnp.swapaxes(patch_taper, 1, 2),
    )
    rows = ens + SUB
    along = [packet] + [turned(packet, signed(x, n_x)) for x in range(1, n_x)]
    halo_list = turned(sent, -1)
    own_tapers = dense_tapers(gz, own_list, 0, patches, mloc, n_x, n_y, slots)
    along = jnp.stack(along, axis=0)
    centred = center(members)
    along = after(along, *own_tapers, *centred)
    beside = [shifted(along, "gy", signed(y, n_y)) for y in range(1, n_y)]
    halo_tapers = dense_tapers(gz, halo_list, -1, patches, mloc, n_x, n_y, slots)
    tapers = own_tapers + halo_tapers
    gram = grams(along, tapers, ens, range(n_x))
    here = jnp.concatenate([along] + after(beside, gram), axis=0)
    there = swapped(here)
    if n_y > 1:
        gram = grams(here[n_x:], tapers, ens, range(n_x, n_x * n_y), gram)
    gram = grams(there, tapers, ens, range(n_x * n_y, 2 * n_x * n_y), gram)
    own = roots(gram, 0, ens)
    pair = swapped(own)
    halo = roots(after(gram, own), 1, ens)
    far = swapped(halo)
    return update(gz, members.shape, centred, own, pair, halo, far)


def solution(mesh):
    return jax.shard_map(
        per_device,
        mesh=mesh,
        in_specs=(
            P("groups", "gz", "gx", "gy"),
            P(("groups", "gz"), "gx", "gy", None),
            P(("groups", "gz"), "gx", "gy", None),
            P(("groups", "gz"), "gx", "gy"),
            P(("groups", "gz"), "gx", "gy", None, None),
            P(("groups", "gz"), "gx", "gy", None, None),
            P(("groups", "gx"), "gy", None),
            P(("groups", "gx"), "gy", None),
        ),
        out_specs=P("groups", "gz", "gx", "gy"),
        check_vma=False,
    )
```

```python
import functools
import math

import jax
import jax.numpy as jnp
from jax import lax
from jax.experimental import pallas as pl
from jax.experimental.pallas import tpu as pltpu
from jax.sharding import PartitionSpec as P

PX = 4
BATCH = 8
F32 = jnp.float32
BF16 = jnp.bfloat16
LANES = 128
SUB = 8
VMEM_LIMIT = 40 << 20
WHOLE_VMEM = (64 << 20) - (256 << 10)


def params(limit=VMEM_LIMIT):
    return pltpu.CompilerParams(vmem_limit_bytes=limit)


def micros(time):
    return pl.CostEstimate(flops=int(time * 1e9), bytes_accessed=int(time * 3e6), transcendentals=0)


def spread(ref, row):
    return ref[pl.ds(row, SUB, stride=0), :]


def block_base(ens):
    nb = ens // SUB
    base, at = [], 0
    for i in range(ens):
        base.append(at)
        at += SUB * (nb - i // SUB)
    return base, at


def observe_kernel(
    gz_ref, count_ref, members_in, cell_in, weight_in, value_in, rinv_in, ids_in, tapers_in,
    out_ref, sent_ref, own_ref,
    members_ref, cell_ref, weight_ref, value_ref, rinv_ref, ids_ref, tapers_ref, wx, pick, part, sems,
):
    ins = (cell_in, weight_in, members_in, value_in, rinv_in, ids_in, tapers_in)
    here = (cell_ref, weight_ref, members_ref, value_ref, rinv_ref, ids_ref, tapers_ref)
    copies = [pltpu.make_async_copy(src, dst, sems.at[n]) for n, (src, dst) in enumerate(zip(ins, here))]
    for copy in copies:
        copy.start()
    copies[0].wait()
    copies[1].wait()
    ens, levels, width_x, width_y = members_ref.shape
    slots = cell_ref.shape[1]
    sten = cell_ref.shape[0]
    cell = cell_ref[...]
    low = jnp.bitwise_and(cell, width_y - 1)
    high = lax.shift_right_logical(cell, width_y.bit_length() - 1)
    low0 = jnp.min(low, axis=0, keepdims=True)
    code = high * 2 + (low - low0)
    weight = weight_ref[...]
    x_iota = lax.broadcasted_iota(jnp.int32, (width_x, slots), 0)
    for level in range(levels):
        for c in range(2):
            want = (level * width_x + x_iota) * 2 + c
            total = jnp.zeros((width_x, slots), F32)
            for s in range(sten):
                total = total + jnp.where(code[s : s + 1] == want, weight[s : s + 1], 0.0)
            wx[c, level * width_x : (level + 1) * width_x, :] = total
    y_iota = lax.broadcasted_iota(jnp.int32, (width_y, slots), 0)
    pick[:, :slots] = jnp.where(y_iota == low0, 1.0, 0.0).astype(BF16)
    pick[:, slots:] = jnp.where(y_iota == low0 + 1, 1.0, 0.0).astype(BF16)
    for copy in copies[3:]:
        copy.wait()
    gz = gz_ref[0]
    own_ref[...] = jnp.concatenate([ids_ref[gz].astype(F32), tapers_ref[gz]], axis=0).T
    sent_ref[...] = jnp.concatenate([ids_ref[1 - gz].astype(F32), tapers_ref[1 - gz]], axis=0).T
    copies[2].wait()

    cells = levels * width_x

    def batch(step, _):
        rows = members_ref[pl.ds(step * BATCH, BATCH)].astype(F32).reshape(BATCH * cells, width_y).astype(BF16)
        got = jnp.dot(rows, pick[...], preferred_element_type=F32)
        for q in range(BATCH):
            total = None
            for at in range(0, cells, SUB):
                row = slice(q * cells + at, q * cells + at + SUB)
                near = slice(at, at + SUB)
                term = got[row, :slots] * wx[0, near] + got[row, slots:] * wx[1, near]
                total = term if at == 0 else total + term
            for half in range(slots // LANES):
                at = pl.ds(pl.multiple_of((step * BATCH + q) * SUB, SUB), SUB)
                part[half, at, :] = total[:, half * LANES : (half + 1) * LANES]
        return 0

    lax.fori_loop(0, ens // BATCH, batch, 0, unroll=True)
    groups = []
    for kb in range(ens // SUB):
        halves = []
        for half in range(slots // LANES):
            total = part[half, pl.ds(kb * SUB * SUB, SUB, stride=SUB), :]
            for s in range(1, SUB):
                total = total + part[half, pl.ds(kb * SUB * SUB + s, SUB, stride=SUB), :]
            halves.append(total)
        groups.append(jnp.concatenate(halves, axis=1))
    total = groups[0]
    for group in groups[1:]:
        total = total + group
    mean = jnp.sum(total, axis=0, keepdims=True) / ens
    for kb in range(ens // SUB):
        out_ref[kb * SUB : (kb + 1) * SUB, :] = groups[kb] - mean
    live = lax.broadcasted_iota(jnp.int32, (1, slots), 1) < count_ref[0]
    innovation = value_ref[...] - mean
    rinv = jnp.where(live, rinv_ref[...], 0.0)
    row = lax.broadcasted_iota(jnp.int32, (SUB, slots), 0)
    out_ref[ens : ens + SUB, :] = jnp.where(row == 0, innovation, jnp.where(row == 1, rinv, 0.0))


def observe(gz, count, members, cell, weight, value, rinv, ids, tapers):
    ens, levels, width_x, width_y = members.shape
    sten, slots = cell.shape
    _, mloc, patches = ids.shape
    vmem = pl.BlockSpec(memory_space=pltpu.VMEM)
    smem = pl.BlockSpec(memory_space=pltpu.SMEM)
    return pl.pallas_call(
        observe_kernel,
        out_shape=(
            jax.ShapeDtypeStruct((ens + SUB, slots), F32),
            jax.ShapeDtypeStruct((patches, 2 * mloc), F32),
            jax.ShapeDtypeStruct((patches, 2 * mloc), F32),
        ),
        in_specs=[smem, smem] + [pl.BlockSpec(memory_space=pltpu.HBM)] * 7,
        out_specs=(vmem, vmem, vmem),
        scratch_shapes=[
            pltpu.VMEM(members.shape, members.dtype),
            pltpu.VMEM(cell.shape, cell.dtype),
            pltpu.VMEM(weight.shape, F32),
            pltpu.VMEM(value.shape, F32),
            pltpu.VMEM(rinv.shape, F32),
            pltpu.VMEM(ids.shape, ids.dtype),
            pltpu.VMEM(tapers.shape, F32),
            pltpu.VMEM((2, levels * width_x, slots), F32),
            pltpu.VMEM((width_y, 2 * slots), BF16),
            pltpu.VMEM((slots // LANES, ens * SUB, LANES), F32),
            pltpu.SemaphoreType.DMA((7,)),
        ],
        compiler_params=params(WHOLE_VMEM),
        cost_estimate=micros(3),
        name="observe",
    )(gz, count, members, cell, weight, value, rinv, ids, tapers)


def taper_kernel(gz_ref, list_ref, high_ref, low_ref, code_s, slot_s, taper_s, *, shift, n_x, n_y, slots, mloc):
    patches = high_ref.shape[1]
    batch = patches // SUB
    gz = gz_ref[0]
    n_buf = 2 * n_x * n_y
    lanes = SUB * mloc
    pairs = [list_ref[pl.ds(q, batch, stride=SUB), :] for q in range(SUB)]
    ids = jnp.concatenate([pair[:, :mloc] for pair in pairs], axis=1).astype(jnp.int32)
    taper = jnp.concatenate([pair[:, mloc:] for pair in pairs], axis=1)
    tile = lax.shift_right_logical(ids, slots.bit_length() - 1)
    upper = (tile >= 9).astype(jnp.int32)
    tile = tile - 9 * upper
    a = (tile >= 3).astype(jnp.int32) + (tile >= 6).astype(jnp.int32)
    b = tile - 3 * a
    other = jnp.where(upper == gz, 0, 1)
    x = jnp.where(gz == 0, a - 1, 1 - a) + shift
    x = lax.rem(jnp.where(other == 0, x, -x) + 2 * n_x, n_x)
    y = lax.rem(b - 1 + n_y, n_y)
    patch = lax.shift_right_logical(lax.broadcasted_iota(jnp.int32, ids.shape, 1), mloc.bit_length() - 1)
    code_s[...] = (((other * n_y + y) * n_x + x) * SUB + patch).astype(F32)
    slot_s[...] = jnp.bitwise_and(ids, slots - 1).astype(F32)
    taper_s[...] = taper
    code_iota = lax.broadcasted_iota(jnp.int32, (n_buf * SUB, lanes), 0).astype(F32).astype(BF16)
    slot_iota = lax.broadcasted_iota(jnp.int32, (slots, lanes), 0).astype(F32).astype(BF16)
    zero, one = jnp.zeros((), BF16), jnp.ones((), BF16)

    def dense(it):
        code = code_s[pl.ds(it, 1), :].astype(BF16)
        slot = slot_s[pl.ds(it, 1), :].astype(BF16)
        taper = taper_s[pl.ds(it, 1), :]
        coarse = taper.astype(BF16)
        fine = (taper - coarse.astype(F32)).astype(BF16)
        hit = code_iota == code
        left = jnp.concatenate([jnp.where(hit, coarse, zero), jnp.where(hit, fine, zero)], axis=0)
        right = jnp.where(slot_iota == slot, one, zero)
        both = lax.dot_general(left, right, (((1,), (1,)), ((), ())), preferred_element_type=F32)
        return both[: n_buf * SUB] + both[n_buf * SUB :]

    def body(it, _):
        first = dense(2 * it)
        second = dense(2 * it + 1)
        for n in range(n_buf):
            rows = slice(n * SUB, (n + 1) * SUB)
            block = jnp.concatenate([first[rows], second[rows]], axis=0)
            high = block.astype(BF16)
            at = pl.ds(pl.multiple_of(it * 2 * SUB, 2 * SUB), 2 * SUB)
            high_ref[n, at, :] = high
            low_ref[n, at, :] = (block - high.astype(F32)).astype(BF16)
        return 0

    lax.fori_loop(0, batch // 2, body, 0, unroll=True)


def dense_tapers(gz, lists, shift, patches, mloc, n_x, n_y, slots):
    vmem = pl.BlockSpec(memory_space=pltpu.VMEM)
    n_buf = 2 * n_x * n_y
    shape = jax.ShapeDtypeStruct((n_buf, patches, slots), BF16)
    batch = patches // SUB
    return pl.pallas_call(
        functools.partial(taper_kernel, shift=shift, n_x=n_x, n_y=n_y, slots=slots, mloc=mloc),
        out_shape=(shape, shape),
        in_specs=[pl.BlockSpec(memory_space=pltpu.SMEM), vmem],
        out_specs=(vmem, vmem),
        scratch_shapes=[
            pltpu.VMEM((batch, SUB * mloc), F32),
            pltpu.VMEM((batch, SUB * mloc), F32),
            pltpu.VMEM((batch, SUB * mloc), F32),
        ],
        compiler_params=params(),
        cost_estimate=micros(3),
        name="dense_tapers",
    )(gz, lists)


def gram_kernel(*refs, ens, bufs, carry):
    refs = list(refs)
    before = refs.pop(0) if carry else None
    stack, own_high, own_low, halo_high, halo_low, out_ref, z_s, zr_s = refs
    nb = ens // SUB
    base, tri = block_base(ens)
    rows = tri + ens
    nt = (((1,), (1,)), ((), ()))
    for t, n in enumerate(bufs):
        ob = stack[t, :ens, :]
        rinv = stack[t, ens + 1 : ens + 2, :]
        zr_s[...] = ob * rinv
        wi = stack[t, ens : ens + 1, :]
        for i in range(0, ens, 2):
            ib = i // SUB
            part = jnp.concatenate(
                [ob[kb * SUB : (kb + 1) * SUB] * zr_s[q : q + 1, :] for q in (i, i + 1) for kb in range(ib, nb)], axis=0
            )
            high = part.astype(BF16)
            z_s[base[i] : base[i] + part.shape[0], :] = high
            z_s[rows + base[i] : rows + base[i] + part.shape[0], :] = (part - high.astype(F32)).astype(BF16)
        part = zr_s[...] * wi
        high = part.astype(BF16)
        z_s[tri:rows, :] = high
        z_s[rows + tri : 2 * rows, :] = (part - high.astype(F32)).astype(BF16)
        right = jnp.concatenate([own_high[n], halo_high[n]], axis=0)
        got = lax.dot_general(z_s[...], right, nt, preferred_element_type=F32)
        right = jnp.concatenate([own_low[n], halo_low[n]], axis=0)
        more = lax.dot_general(z_s[:rows, :], right, nt, preferred_element_type=F32)
        total = got[:rows] + (got[rows:] + more)
        if t > 0:
            total = out_ref[...] + total
        elif carry:
            total = before[...] + total
        out_ref[...] = total


def grams(stack, tapers, ens, bufs, before=None):
    vmem = pl.BlockSpec(memory_space=pltpu.VMEM)
    _, tri = block_base(ens)
    rows = tri + ens
    _, patches, slots = tapers[0].shape
    carry = before is not None
    args = ((before,) if carry else ()) + (stack,) + tuple(tapers)
    return pl.pallas_call(
        functools.partial(gram_kernel, ens=ens, bufs=tuple(bufs), carry=carry),
        out_shape=jax.ShapeDtypeStruct((rows, 2 * patches), F32),
        in_specs=[vmem] * len(args),
        out_specs=vmem,
        scratch_shapes=[pltpu.VMEM((2 * rows, slots), BF16), pltpu.VMEM((ens, slots), F32)],
        compiler_params=params(),
        cost_estimate=micros(2),
        name="grams",
    )(*args)


def product(ens, a, b, dests, epilogue):
    nb = ens // SUB
    for ib in range(nb):
        n = nb - ib
        rows = 4 if n > 2 else 8

        def body(step, _, ib=ib, n=n, rows=rows):
            i0 = ib * SUB + step * rows
            acc = [[None] * n for _ in range(rows)]
            for j in range(ens):
                right = [b[j * ens + SUB * kb : j * ens + SUB * (kb + 1), :] for kb in range(ib, nb)]
                for ii in range(rows):
                    left = spread(a, (i0 + ii) * ens + j)
                    for q in range(n):
                        term = left * right[q]
                        acc[ii][q] = term if j == 0 else acc[ii][q] + term
            for ii in range(rows):
                for q in range(n):
                    kb = ib + q
                    eye = None
                    if q == 0:
                        eye = lax.broadcasted_iota(jnp.int32, (SUB, LANES), 0) == step * rows + ii
                    outs = epilogue(acc[ii][q], pl.ds((i0 + ii) * ens + SUB * kb, SUB), eye)
                    for dest, value in zip(dests, outs):
                        dest[pl.ds((i0 + ii) * ens + SUB * kb, SUB), :] = value
                        if kb > ib:
                            dest[pl.ds(SUB * kb * ens + i0 + ii, SUB, stride=ens), :] = value
            return 0

        lax.fori_loop(0, SUB // rows, body, 0, unroll=True)


def root_kernel(gram_ref, out_ref, s_a, s_b, s_c, s_d, vec, *, ens, row):
    nb = ens // SUB
    base, tri = block_base(ens)
    lanes = slice(row * LANES, (row + 1) * LANES)
    diag = gram_ref[0:1, lanes]
    for i in range(1, ens):
        at = base[i] + i % SUB
        diag = diag + gram_ref[at : at + 1, lanes]
    half = 0.5 * (diag + (ens - 1.0) * ens)
    scale = jnp.broadcast_to(1.0 / half, (SUB, LANES))
    iota = lax.broadcasted_iota(jnp.int32, (SUB, LANES), 0)
    for i in range(ens):
        for kb in range(i // SUB, nb):
            at = base[i] + SUB * (kb - i // SUB)
            value = gram_ref[at : at + SUB, lanes]
            if kb == i // SUB:
                value = jnp.where(iota == i % SUB, value + (ens - 1.0), value)
            value = value * scale
            s_a[i * ens + SUB * kb : i * ens + SUB * (kb + 1), :] = value
            if kb > i // SUB:
                s_a[pl.ds(SUB * kb * ens + i, SUB, stride=ens), :] = value

    def plain(acc, at, eye):
        return (acc,)

    def quadratic(lin):
        def epilogue(acc, at, eye):
            rest = 0.0625 * acc - 0.5625 * lin[at, :]
            if eye is not None:
                rest = jnp.where(eye, rest + 1.6875, rest)
            return (acc, rest)

        return epilogue

    def quartic(lin):
        def epilogue(acc, at, eye):
            rest = acc - 2.4375 * lin[at, :]
            if eye is not None:
                rest = jnp.where(eye, rest + 2.25, rest)
            return (rest,)

        return epilogue

    product(ens, s_a, s_a, (s_b, s_c), quadratic(s_a))
    product(ens, s_b, s_c, (s_d,), quartic(s_a))
    product(ens, s_d, s_d, (s_b,), plain)
    product(ens, s_a, s_b, (s_c,), plain)
    product(ens, s_c, s_c, (s_a, s_b), quadratic(s_c))
    product(ens, s_a, s_b, (vec.at[pl.ds(0, ens * ens)],), quartic(s_c))
    product(ens, s_d, vec.at[pl.ds(0, ens * ens)], (s_a,), plain)

    right = ens * ens
    vec[right : right + ens, :] = gram_ref[tri : tri + ens, lanes]

    def apply(source):
        sums = [None] * nb
        for i in range(ens):
            left = spread(vec, source + i)
            for kb in range(nb):
                term = left * s_a[i * ens + SUB * kb : i * ens + SUB * (kb + 1), :]
                sums[kb] = term if i == 0 else sums[kb] + term
        return sums

    inner = apply(right)
    for kb in range(nb):
        vec[right + ens + SUB * kb : right + ens + SUB * (kb + 1), :] = inner[kb]
    outer = apply(right + ens)
    for kb in range(nb):
        vec[right + SUB * kb : right + SUB * (kb + 1), :] = outer[kb] * scale
    factor = jnp.broadcast_to(math.sqrt(ens - 1.0) / jnp.sqrt(half), (SUB, LANES))
    for j in range(ens):
        weight = spread(vec, right + j)
        for kb in range(nb):
            at = slice(j * ens + SUB * kb, j * ens + SUB * (kb + 1))
            out_ref[at, :] = weight + s_a[at, :] * factor


def roots(gram, row, ens):
    square = pltpu.VMEM((ens * ens, LANES), F32)
    vmem = pl.BlockSpec(memory_space=pltpu.VMEM)
    return pl.pallas_call(
        functools.partial(root_kernel, ens=ens, row=row),
        out_shape=jax.ShapeDtypeStruct((ens * ens, LANES), F32),
        in_specs=[vmem],
        out_specs=vmem,
        scratch_shapes=[square] * 4 + [pltpu.VMEM((ens * ens + 2 * ens, LANES), F32)],
        compiler_params=params(),
        cost_estimate=micros(7),
        name="roots",
    )(gram)


def center_kernel(members_ref, pert_ref, mean_ref):
    ens, levels, width_x, _ = members_ref.shape
    for level in range(levels):
        total = members_ref[0, level].astype(F32)
        for k in range(1, ens):
            total = total + members_ref[k, level].astype(F32)
        mean = total / ens
        mean_ref[level * width_x : (level + 1) * width_x, :] = mean
        for k in range(ens):
            at = (k * levels + level) * width_x
            pert_ref[at : at + width_x, :] = members_ref[k, level].astype(F32) - mean


def center(members):
    ens, levels, width_x, width_y = members.shape
    vmem = pl.BlockSpec(memory_space=pltpu.VMEM)
    cells = levels * width_x
    return pl.pallas_call(
        center_kernel,
        out_shape=(
            jax.ShapeDtypeStruct((ens * cells, width_y), F32),
            jax.ShapeDtypeStruct((cells, width_y), F32),
        ),
        in_specs=[vmem],
        out_specs=(vmem, vmem),
        compiler_params=params(),
        cost_estimate=micros(1),
        name="center",
    )(members)


def columns(gz, pert_ref, mean_ref, dest, main_ref, beside_ref, first, ens, levels, width_x):
    nb = ens // SUB
    near = first % PX

    def body(step, _):
        place = jnp.abs((near + step + 0.5) / PX - 0.5)
        turned_x = first + step
        x = jnp.where(gz == 0, turned_x, width_x - 1 - turned_x)
        w_main = jnp.broadcast_to(1.0 - place, (SUB, LANES))
        w_beside = jnp.broadcast_to(place, (SUB, LANES))
        acc = [[spread(mean_ref, level * width_x + x)] * nb for level in range(levels)]
        for j in range(ens):
            blend = []
            for kb in range(nb):
                at = slice(j * ens + SUB * kb, j * ens + SUB * (kb + 1))
                blend.append(w_main * main_ref[at, :] + w_beside * beside_ref[at, :])
            for level in range(levels):
                pert = spread(pert_ref, (j * levels + level) * width_x + x)
                for kb in range(nb):
                    acc[level][kb] = acc[level][kb] + pert * blend[kb]
        for level in range(levels):
            for kb in range(nb):
                at = (SUB * kb * levels + level) * width_x + x
                dest[pl.ds(at, SUB, stride=levels * width_x), :] = acc[level][kb]
        return 0

    lax.fori_loop(0, PX // 2, body, 0)


def inner_kernel(gz_ref, pert_ref, mean_ref, own_ref, pair_ref, halo_ref, part_ref, *, ens, levels, width_x):
    gz = gz_ref[0]
    sizes = (ens, levels, width_x)
    columns(gz, pert_ref, mean_ref, part_ref, own_ref, halo_ref, 0, *sizes)
    columns(gz, pert_ref, mean_ref, part_ref, own_ref, pair_ref, PX // 2, *sizes)
    columns(gz, pert_ref, mean_ref, part_ref, pair_ref, own_ref, PX, *sizes)


def outer_kernel(gz_ref, pert_ref, mean_ref, pair_ref, far_ref, part_ref, out_ref, rest_s):
    ens, levels, width_x, width_y = out_ref.shape
    gz = gz_ref[0]
    first = 3 * PX // 2
    columns(gz, pert_ref, mean_ref, rest_s, pair_ref, far_ref, first, ens, levels, width_x)
    x = lax.broadcasted_iota(jnp.int32, (width_x, width_y), 0)
    inside = jnp.where(gz == 0, x, width_x - 1 - x) < first
    for k in range(ens):
        for level in range(levels):
            at = slice((k * levels + level) * width_x, (k * levels + level + 1) * width_x)
            out_ref[k, level] = jnp.where(inside, part_ref[at, :], rest_s[at, :]).astype(BF16)


def update(gz, shape, centred, own, pair, halo, far):
    ens, levels, width_x, width_y = shape
    pert, mean = centred
    vmem = pl.BlockSpec(memory_space=pltpu.VMEM)
    smem = pl.BlockSpec(memory_space=pltpu.SMEM)
    part = pl.pallas_call(
        functools.partial(inner_kernel, ens=ens, levels=levels, width_x=width_x),
        out_shape=jax.ShapeDtypeStruct(pert.shape, F32),
        in_specs=[smem] + [vmem] * 5,
        out_specs=vmem,
        compiler_params=params(),
        cost_estimate=micros(3),
        name="inner",
    )(gz, pert, mean, own, pair, halo)
    return pl.pallas_call(
        outer_kernel,
        out_shape=jax.ShapeDtypeStruct(shape, BF16),
        in_specs=[smem] + [vmem] * 5,
        out_specs=vmem,
        scratch_shapes=[pltpu.VMEM(pert.shape, F32)],
        compiler_params=params(),
        cost_estimate=micros(1),
        name="outer",
    )(gz, pert, mean, pair, far, part)


def shifted(x, axis, shift):
    size = lax.axis_size(axis)
    return lax.ppermute(x, axis, [((i + shift) % size, i) for i in range(size)])


def turned(x, shift):
    size = lax.axis_size("gx")
    pairs = [(2 * ((i + shift) % size), 2 * i) for i in range(size)]
    pairs += [(2 * ((i - shift) % size) + 1, 2 * i + 1) for i in range(size)]
    return lax.ppermute(x, ("gx", "gz"), pairs)


def swapped(x):
    return lax.ppermute(x, "gz", [(0, 1), (1, 0)])


def signed(index, count):
    return index if index <= count // 2 else index - count


def after(x, *others):
    return lax.optimization_barrier((x,) + others)[0]


def per_device(
    members, obs_value, obs_rinv, obs_count, stencil_cell, stencil_weight, patch_list, patch_taper
):
    ens = members.shape[0]
    slots = obs_value.shape[-1]
    _, patches, mloc = patch_list.shape
    size_x, size_y = lax.axis_size("gx"), lax.axis_size("gy")
    n_x, n_y = min(size_x, 5), min(size_y, 3)
    gz = lax.axis_index("gz").reshape(1).astype(jnp.int32)
    packet, sent, own_list = observe(
        gz,
        obs_count.reshape(1),
        members,
        stencil_cell.reshape(-1, slots),
        stencil_weight.reshape(-1, slots),
        obs_value.reshape(1, slots),
        obs_rinv.reshape(1, slots),
        jnp.swapaxes(patch_list, 1, 2),
        jnp.swapaxes(patch_taper, 1, 2),
    )
    rows = ens + SUB
    along = [packet] + [turned(packet, signed(x, n_x)) for x in range(1, n_x)]
    halo_list = turned(sent, -1)
    own_tapers = dense_tapers(gz, own_list, 0, patches, mloc, n_x, n_y, slots)
    along = jnp.stack(along, axis=0)
    centred = center(members)
    along = after(along, *own_tapers, *centred)
    beside = [shifted(along, "gy", signed(y, n_y)) for y in range(1, n_y)]
    halo_tapers = dense_tapers(gz, halo_list, -1, patches, mloc, n_x, n_y, slots)
    tapers = own_tapers + halo_tapers
    gram = grams(along, tapers, ens, range(n_x))
    here = jnp.concatenate([along] + after(beside, gram), axis=0)
    there = swapped(here)
    if n_y > 1:
        gram = grams(here[n_x:], tapers, ens, range(n_x, n_x * n_y), gram)
    gram = grams(there, tapers, ens, range(n_x * n_y, 2 * n_x * n_y), gram)
    own = roots(gram, 0, ens)
    pair = swapped(own)
    halo = roots(after(gram, own), 1, ens)
    far = swapped(halo)
    return update(gz, members.shape, centred, own, pair, halo, far)


def solution(mesh):
    return jax.shard_map(
        per_device,
        mesh=mesh,
        in_specs=(
            P("groups", "gz", "gx", "gy"),
            P(("groups", "gz"), "gx", "gy", None),
            P(("groups", "gz"), "gx", "gy", None),
            P(("groups", "gz"), "gx", "gy"),
            P(("groups", "gz"), "gx", "gy", None, None),
            P(("groups", "gz"), "gx", "gy", None, None),
            P(("groups", "gx"), "gy", None),
            P(("groups", "gx"), "gy", None),
        ),
        out_specs=P("groups", "gz", "gx", "gy"),
        check_vma=False,
    )
```

```python
import functools
import math

import jax
import jax.numpy as jnp
from jax import lax
from jax.experimental import pallas as pl
from jax.experimental.pallas import tpu as pltpu
from jax.sharding import PartitionSpec as P

PX = 4
PIT = 40
BATCH = 8
F32 = jnp.float32
BF16 = jnp.bfloat16
LANES = 128
SUB = 8
VMEM_LIMIT = 40 << 20
WHOLE_VMEM = (64 << 20) - (256 << 10)


def params(limit=VMEM_LIMIT):
    return pltpu.CompilerParams(vmem_limit_bytes=limit)


def micros(time):
    return pl.CostEstimate(flops=int(time * 1e9), bytes_accessed=int(time * 3e6), transcendentals=0)


def spread(ref, row):
    return ref[pl.ds(row, SUB, stride=0), :]


def block_base(ens):
    nb = ens // SUB
    base, at = [], 0
    for i in range(ens):
        base.append(at)
        at += SUB * (nb - i // SUB)
    return base, at


def observe_kernel(
    gz_ref, count_ref, members_in, cell_in, weight_in, value_in, rinv_in, ids_in, tapers_in,
    out_ref, sent_ref, own_ref,
    members_ref, cell_ref, weight_ref, value_ref, rinv_ref, ids_ref, tapers_ref, wx, pick, part, sems,
):
    ins = (cell_in, weight_in, members_in, value_in, rinv_in, ids_in, tapers_in)
    here = (cell_ref, weight_ref, members_ref, value_ref, rinv_ref, ids_ref, tapers_ref)
    copies = [pltpu.make_async_copy(src, dst, sems.at[n]) for n, (src, dst) in enumerate(zip(ins, here))]
    for copy in copies:
        copy.start()
    copies[0].wait()
    copies[1].wait()
    ens, levels, width_x, width_y = members_ref.shape
    slots = cell_ref.shape[1]
    sten = cell_ref.shape[0]
    cell = cell_ref[...]
    low = jnp.bitwise_and(cell, width_y - 1)
    high = lax.shift_right_logical(cell, width_y.bit_length() - 1)
    low0 = jnp.min(low, axis=0, keepdims=True)
    code = high * 2 + (low - low0)
    weight = weight_ref[...]
    x_iota = lax.broadcasted_iota(jnp.int32, (width_x, slots), 0)
    for level in range(levels):
        for c in range(2):
            want = (level * width_x + x_iota) * 2 + c
            total = jnp.zeros((width_x, slots), F32)
            for s in range(sten):
                total = total + jnp.where(code[s : s + 1] == want, weight[s : s + 1], 0.0)
            wx[c, level * width_x : (level + 1) * width_x, :] = total
    y_iota = lax.broadcasted_iota(jnp.int32, (width_y, slots), 0)
    pick[:, :slots] = jnp.where(y_iota == low0, 1.0, 0.0).astype(BF16)
    pick[:, slots:] = jnp.where(y_iota == low0 + 1, 1.0, 0.0).astype(BF16)
    for copy in copies[3:]:
        copy.wait()
    gz = gz_ref[0]
    own_ref[...] = jnp.concatenate([ids_ref[gz].astype(F32), tapers_ref[gz]], axis=0).T
    sent_ref[...] = jnp.concatenate([ids_ref[1 - gz].astype(F32), tapers_ref[1 - gz]], axis=0).T
    copies[2].wait()

    cells = levels * width_x

    def batch(step, _):
        rows = members_ref[pl.ds(step * BATCH, BATCH)].astype(F32).reshape(BATCH * cells, width_y).astype(BF16)
        got = jnp.dot(rows, pick[...], preferred_element_type=F32)
        for q in range(BATCH):
            total = None
            for at in range(0, cells, SUB):
                row = slice(q * cells + at, q * cells + at + SUB)
                near = slice(at, at + SUB)
                term = got[row, :slots] * wx[0, near] + got[row, slots:] * wx[1, near]
                total = term if at == 0 else total + term
            for half in range(slots // LANES):
                at = pl.ds(pl.multiple_of((step * BATCH + q) * SUB, SUB), SUB)
                part[half, at, :] = total[:, half * LANES : (half + 1) * LANES]
        return 0

    lax.fori_loop(0, ens // BATCH, batch, 0, unroll=True)
    groups = []
    for kb in range(ens // SUB):
        halves = []
        for half in range(slots // LANES):
            total = part[half, pl.ds(kb * SUB * SUB, SUB, stride=SUB), :]
            for s in range(1, SUB):
                total = total + part[half, pl.ds(kb * SUB * SUB + s, SUB, stride=SUB), :]
            halves.append(total)
        groups.append(jnp.concatenate(halves, axis=1))
    total = groups[0]
    for group in groups[1:]:
        total = total + group
    mean = jnp.sum(total, axis=0, keepdims=True) / ens
    for kb in range(ens // SUB):
        out_ref[kb * SUB : (kb + 1) * SUB, :] = groups[kb] - mean
    live = lax.broadcasted_iota(jnp.int32, (1, slots), 1) < count_ref[0]
    innovation = value_ref[...] - mean
    rinv = jnp.where(live, rinv_ref[...], 0.0)
    row = lax.broadcasted_iota(jnp.int32, (SUB, slots), 0)
    out_ref[ens : ens + SUB, :] = jnp.where(row == 0, innovation, jnp.where(row == 1, rinv, 0.0))


def observe(gz, count, members, cell, weight, value, rinv, ids, tapers):
    ens, levels, width_x, width_y = members.shape
    sten, slots = cell.shape
    _, mloc, patches = ids.shape
    vmem = pl.BlockSpec(memory_space=pltpu.VMEM)
    smem = pl.BlockSpec(memory_space=pltpu.SMEM)
    return pl.pallas_call(
        observe_kernel,
        out_shape=(
            jax.ShapeDtypeStruct((ens + SUB, slots), F32),
            jax.ShapeDtypeStruct((patches, 2 * mloc), F32),
            jax.ShapeDtypeStruct((patches, 2 * mloc), F32),
        ),
        in_specs=[smem, smem] + [pl.BlockSpec(memory_space=pltpu.HBM)] * 7,
        out_specs=(vmem, vmem, vmem),
        scratch_shapes=[
            pltpu.VMEM(members.shape, members.dtype),
            pltpu.VMEM(cell.shape, cell.dtype),
            pltpu.VMEM(weight.shape, F32),
            pltpu.VMEM(value.shape, F32),
            pltpu.VMEM(rinv.shape, F32),
            pltpu.VMEM(ids.shape, ids.dtype),
            pltpu.VMEM(tapers.shape, F32),
            pltpu.VMEM((2, levels * width_x, slots), F32),
            pltpu.VMEM((width_y, 2 * slots), BF16),
            pltpu.VMEM((slots // LANES, ens * SUB, LANES), F32),
            pltpu.SemaphoreType.DMA((7,)),
        ],
        compiler_params=params(WHOLE_VMEM),
        cost_estimate=micros(3),
        name="observe",
    )(gz, count, members, cell, weight, value, rinv, ids, tapers)


def taper_kernel(gz_ref, list_ref, high_ref, low_ref, code_s, slot_s, taper_s, *, shift, n_x, n_y, slots, mloc):
    patches = high_ref.shape[1]
    batch = patches // SUB
    gz = gz_ref[0]
    n_buf = 2 * n_x * n_y
    lanes = SUB * mloc
    pairs = [list_ref[pl.ds(q, batch, stride=SUB), :] for q in range(SUB)]
    ids = jnp.concatenate([pair[:, :mloc] for pair in pairs], axis=1).astype(jnp.int32)
    taper = jnp.concatenate([pair[:, mloc:] for pair in pairs], axis=1)
    tile = lax.shift_right_logical(ids, slots.bit_length() - 1)
    upper = (tile >= 9).astype(jnp.int32)
    tile = tile - 9 * upper
    a = (tile >= 3).astype(jnp.int32) + (tile >= 6).astype(jnp.int32)
    b = tile - 3 * a
    other = jnp.where(upper == gz, 0, 1)
    x = jnp.where(gz == 0, a - 1, 1 - a) + shift
    x = lax.rem(jnp.where(other == 0, x, -x) + 2 * n_x, n_x)
    y = lax.rem(b - 1 + n_y, n_y)
    patch = lax.shift_right_logical(lax.broadcasted_iota(jnp.int32, ids.shape, 1), mloc.bit_length() - 1)
    code_s[...] = (((other * n_y + y) * n_x + x) * SUB + patch).astype(F32)
    slot_s[...] = jnp.bitwise_and(ids, slots - 1).astype(F32)
    taper_s[...] = taper
    code_iota = lax.broadcasted_iota(jnp.int32, (n_buf * SUB, lanes), 0).astype(F32).astype(BF16)
    slot_iota = lax.broadcasted_iota(jnp.int32, (slots, lanes), 0).astype(F32).astype(BF16)
    zero, one = jnp.zeros((), BF16), jnp.ones((), BF16)

    def dense(it):
        code = code_s[pl.ds(it, 1), :].astype(BF16)
        slot = slot_s[pl.ds(it, 1), :].astype(BF16)
        taper = taper_s[pl.ds(it, 1), :]
        coarse = taper.astype(BF16)
        fine = (taper - coarse.astype(F32)).astype(BF16)
        hit = code_iota == code
        left = jnp.concatenate([jnp.where(hit, coarse, zero), jnp.where(hit, fine, zero)], axis=0)
        right = jnp.where(slot_iota == slot, one, zero)
        both = lax.dot_general(left, right, (((1,), (1,)), ((), ())), preferred_element_type=F32)
        return both[: n_buf * SUB] + both[n_buf * SUB :]

    def body(it, _):
        first = dense(2 * it)
        second = dense(2 * it + 1)
        for n in range(n_buf):
            rows = slice(n * SUB, (n + 1) * SUB)
            block = jnp.concatenate([first[rows], second[rows]], axis=0)
            high = block.astype(BF16)
            at = pl.ds(pl.multiple_of(it * 2 * SUB, 2 * SUB), 2 * SUB)
            high_ref[n, at, :] = high
            low_ref[n, at, :] = (block - high.astype(F32)).astype(BF16)
        return 0

    lax.fori_loop(0, batch // 2, body, 0, unroll=True)


def dense_tapers(gz, lists, shift, patches, mloc, n_x, n_y, slots):
    vmem = pl.BlockSpec(memory_space=pltpu.VMEM)
    n_buf = 2 * n_x * n_y
    shape = jax.ShapeDtypeStruct((n_buf, patches, slots), BF16)
    batch = patches // SUB
    return pl.pallas_call(
        functools.partial(taper_kernel, shift=shift, n_x=n_x, n_y=n_y, slots=slots, mloc=mloc),
        out_shape=(shape, shape),
        in_specs=[pl.BlockSpec(memory_space=pltpu.SMEM), vmem],
        out_specs=(vmem, vmem),
        scratch_shapes=[
            pltpu.VMEM((batch, SUB * mloc), F32),
            pltpu.VMEM((batch, SUB * mloc), F32),
            pltpu.VMEM((batch, SUB * mloc), F32),
        ],
        compiler_params=params(),
        cost_estimate=micros(3),
        name="dense_tapers",
    )(gz, lists)


def gram_kernel(*refs, ens, bufs, carry):
    refs = list(refs)
    before = refs.pop(0) if carry else None
    stack, own_high, own_low, halo_high, halo_low, out_ref, z_s, zr_s = refs
    nb = ens // SUB
    base, tri = block_base(ens)
    rows = tri + ens
    nt = (((1,), (1,)), ((), ()))
    for t, n in enumerate(bufs):
        ob = stack[t, :ens, :]
        rinv = stack[t, ens + 1 : ens + 2, :]
        zr_s[...] = ob * rinv
        wi = stack[t, ens : ens + 1, :]
        for i in range(0, ens, 2):
            ib = i // SUB
            part = jnp.concatenate(
                [ob[kb * SUB : (kb + 1) * SUB] * zr_s[q : q + 1, :] for q in (i, i + 1) for kb in range(ib, nb)], axis=0
            )
            high = part.astype(BF16)
            z_s[base[i] : base[i] + part.shape[0], :] = high
            z_s[rows + base[i] : rows + base[i] + part.shape[0], :] = (part - high.astype(F32)).astype(BF16)
        part = zr_s[...] * wi
        high = part.astype(BF16)
        z_s[tri:rows, :] = high
        z_s[rows + tri : 2 * rows, :] = (part - high.astype(F32)).astype(BF16)
        right = jnp.concatenate([own_high[n], halo_high[n]], axis=0)
        got = lax.dot_general(z_s[...], right, nt, preferred_element_type=F32)
        right = jnp.concatenate([own_low[n], halo_low[n]], axis=0)
        more = lax.dot_general(z_s[:rows, :], right, nt, preferred_element_type=F32)
        total = got[:rows] + (got[rows:] + more)
        if t > 0:
            total = out_ref[...] + total
        elif carry:
            total = before[...] + total
        out_ref[...] = total


def grams(stack, tapers, ens, bufs, before=None):
    vmem = pl.BlockSpec(memory_space=pltpu.VMEM)
    _, tri = block_base(ens)
    rows = tri + ens
    _, patches, slots = tapers[0].shape
    carry = before is not None
    args = ((before,) if carry else ()) + (stack,) + tuple(tapers)
    return pl.pallas_call(
        functools.partial(gram_kernel, ens=ens, bufs=tuple(bufs), carry=carry),
        out_shape=jax.ShapeDtypeStruct((rows, 2 * patches), F32),
        in_specs=[vmem] * len(args),
        out_specs=vmem,
        scratch_shapes=[pltpu.VMEM((2 * rows, slots), BF16), pltpu.VMEM((ens, slots), F32)],
        compiler_params=params(),
        cost_estimate=micros(2),
        name="grams",
    )(*args)


def product(ens, a, b, dests, epilogue):
    nb = ens // SUB
    for ib in range(nb):
        n = nb - ib
        rows = 4 if n > 2 else 8

        def body(step, _, ib=ib, n=n, rows=rows):
            i0 = ib * SUB + step * rows
            acc = [[None] * n for _ in range(rows)]
            for j in range(ens):
                right = [b[j * PIT + SUB * kb : j * PIT + SUB * (kb + 1), :] for kb in range(ib, nb)]
                for ii in range(rows):
                    left = spread(a, (i0 + ii) * PIT + j)
                    for q in range(n):
                        term = left * right[q]
                        acc[ii][q] = term if j == 0 else acc[ii][q] + term
            for ii in range(rows):
                for q in range(n):
                    kb = ib + q
                    eye = None
                    if q == 0:
                        eye = lax.broadcasted_iota(jnp.int32, (SUB, LANES), 0) == step * rows + ii
                    outs = epilogue(acc[ii][q], pl.ds((i0 + ii) * PIT + SUB * kb, SUB), eye)
                    for dest, value in zip(dests, outs):
                        dest[pl.ds((i0 + ii) * PIT + SUB * kb, SUB), :] = value
                        if kb > ib:
                            dest[pl.ds(SUB * kb * PIT + i0 + ii, SUB, stride=PIT), :] = value
            return 0

        lax.fori_loop(0, SUB // rows, body, 0, unroll=True)


def root_kernel(gram_ref, out_ref, s_a, s_b, s_c, s_d, vec, *, ens, row):
    nb = ens // SUB
    base, tri = block_base(ens)
    lanes = slice(row * LANES, (row + 1) * LANES)
    diag = gram_ref[0:1, lanes]
    for i in range(1, ens):
        at = base[i] + i % SUB
        diag = diag + gram_ref[at : at + 1, lanes]
    half = 0.5 * (diag + (ens - 1.0) * ens)
    scale = jnp.broadcast_to(1.0 / half, (SUB, LANES))
    iota = lax.broadcasted_iota(jnp.int32, (SUB, LANES), 0)
    for i in range(ens):
        for kb in range(i // SUB, nb):
            at = base[i] + SUB * (kb - i // SUB)
            value = gram_ref[at : at + SUB, lanes]
            if kb == i // SUB:
                value = jnp.where(iota == i % SUB, value + (ens - 1.0), value)
            value = value * scale
            s_a[i * PIT + SUB * kb : i * PIT + SUB * (kb + 1), :] = value
            if kb > i // SUB:
                s_a[pl.ds(SUB * kb * PIT + i, SUB, stride=PIT), :] = value

    def plain(acc, at, eye):
        return (acc,)

    def quadratic(lin):
        def epilogue(acc, at, eye):
            rest = 0.0625 * acc - 0.5625 * lin[at, :]
            if eye is not None:
                rest = jnp.where(eye, rest + 1.6875, rest)
            return (acc, rest)

        return epilogue

    def quartic(lin):
        def epilogue(acc, at, eye):
            rest = acc - 2.4375 * lin[at, :]
            if eye is not None:
                rest = jnp.where(eye, rest + 2.25, rest)
            return (rest,)

        return epilogue

    product(ens, s_a, s_a, (s_b, s_c), quadratic(s_a))
    product(ens, s_b, s_c, (s_d,), quartic(s_a))
    product(ens, s_d, s_d, (s_b,), plain)
    product(ens, s_a, s_b, (s_c,), plain)
    product(ens, s_c, s_c, (s_a, s_b), quadratic(s_c))
    product(ens, s_a, s_b, (vec.at[pl.ds(0, ens * PIT)],), quartic(s_c))
    product(ens, s_d, vec.at[pl.ds(0, ens * PIT)], (s_a,), plain)

    right = ens * PIT
    vec[right : right + ens, :] = gram_ref[tri : tri + ens, lanes]

    def apply(source):
        sums = [None] * nb
        for i in range(ens):
            left = spread(vec, source + i)
            for kb in range(nb):
                term = left * s_a[i * PIT + SUB * kb : i * PIT + SUB * (kb + 1), :]
                sums[kb] = term if i == 0 else sums[kb] + term
        return sums

    inner = apply(right)
    for kb in range(nb):
        vec[right + ens + SUB * kb : right + ens + SUB * (kb + 1), :] = inner[kb]
    outer = apply(right + ens)
    for kb in range(nb):
        vec[right + SUB * kb : right + SUB * (kb + 1), :] = outer[kb] * scale
    factor = jnp.broadcast_to(math.sqrt(ens - 1.0) / jnp.sqrt(half), (SUB, LANES))
    for j in range(ens):
        weight = spread(vec, right + j)
        for kb in range(nb):
            at = slice(j * PIT + SUB * kb, j * PIT + SUB * (kb + 1))
            out_ref[j * ens + SUB * kb : j * ens + SUB * (kb + 1), :] = weight + s_a[at, :] * factor


def roots(gram, row, ens):
    square = pltpu.VMEM((ens * PIT, LANES), F32)
    vmem = pl.BlockSpec(memory_space=pltpu.VMEM)
    return pl.pallas_call(
        functools.partial(root_kernel, ens=ens, row=row),
        out_shape=jax.ShapeDtypeStruct((ens * ens, LANES), F32),
        in_specs=[vmem],
        out_specs=vmem,
        scratch_shapes=[square] * 4 + [pltpu.VMEM((ens * PIT + 2 * ens, LANES), F32)],
        compiler_params=params(),
        cost_estimate=micros(7),
        name="roots",
    )(gram)


def center_kernel(members_ref, pert_ref, mean_ref):
    ens, levels, width_x, _ = members_ref.shape
    for level in range(levels):
        total = members_ref[0, level].astype(F32)
        for k in range(1, ens):
            total = total + members_ref[k, level].astype(F32)
        mean = total / ens
        mean_ref[level * width_x : (level + 1) * width_x, :] = mean
        for k in range(ens):
            at = (k * levels + level) * width_x
            pert_ref[at : at + width_x, :] = members_ref[k, level].astype(F32) - mean


def center(members):
    ens, levels, width_x, width_y = members.shape
    vmem = pl.BlockSpec(memory_space=pltpu.VMEM)
    cells = levels * width_x
    return pl.pallas_call(
        center_kernel,
        out_shape=(
            jax.ShapeDtypeStruct((ens * cells, width_y), F32),
            jax.ShapeDtypeStruct((cells, width_y), F32),
        ),
        in_specs=[vmem],
        out_specs=(vmem, vmem),
        compiler_params=params(),
        cost_estimate=micros(1),
        name="center",
    )(members)


def columns(gz, pert_ref, mean_ref, dest, main_ref, beside_ref, first, ens, levels, width_x):
    nb = ens // SUB
    near = first % PX
    step_k = levels * width_x + SUB

    def body(step, _):
        place = jnp.abs((near + step + 0.5) / PX - 0.5)
        turned_x = first + step
        x = jnp.where(gz == 0, turned_x, width_x - 1 - turned_x)
        w_main = jnp.broadcast_to(1.0 - place, (SUB, LANES))
        w_beside = jnp.broadcast_to(place, (SUB, LANES))
        acc = [[spread(mean_ref, level * width_x + x)] * nb for level in range(levels)]
        for j in range(ens):
            blend = []
            for kb in range(nb):
                at = slice(j * ens + SUB * kb, j * ens + SUB * (kb + 1))
                blend.append(w_main * main_ref[at, :] + w_beside * beside_ref[at, :])
            for level in range(levels):
                pert = spread(pert_ref, (j * levels + level) * width_x + x)
                for kb in range(nb):
                    acc[level][kb] = acc[level][kb] + pert * blend[kb]
        for level in range(levels):
            for kb in range(nb):
                at = SUB * kb * step_k + level * width_x + x
                dest[pl.ds(at, SUB, stride=step_k), :] = acc[level][kb]
        return 0

    lax.fori_loop(0, PX // 2, body, 0)


def inner_kernel(gz_ref, pert_ref, mean_ref, own_ref, pair_ref, halo_ref, part_ref, *, ens, levels, width_x):
    gz = gz_ref[0]
    sizes = (ens, levels, width_x)
    columns(gz, pert_ref, mean_ref, part_ref, own_ref, halo_ref, 0, *sizes)
    columns(gz, pert_ref, mean_ref, part_ref, own_ref, pair_ref, PX // 2, *sizes)
    columns(gz, pert_ref, mean_ref, part_ref, pair_ref, own_ref, PX, *sizes)


def outer_kernel(gz_ref, pert_ref, mean_ref, pair_ref, far_ref, part_ref, out_ref, rest_s):
    ens, levels, width_x, width_y = out_ref.shape
    gz = gz_ref[0]
    first = 3 * PX // 2
    step_k = levels * width_x + SUB
    columns(gz, pert_ref, mean_ref, rest_s, pair_ref, far_ref, first, ens, levels, width_x)
    x = lax.broadcasted_iota(jnp.int32, (width_x, width_y), 0)
    inside = jnp.where(gz == 0, x, width_x - 1 - x) < first
    for k in range(ens):
        for level in range(levels):
            at = slice(k * step_k + level * width_x, k * step_k + (level + 1) * width_x)
            out_ref[k, level] = jnp.where(inside, part_ref[at, :], rest_s[at, :]).astype(BF16)


def update(gz, shape, centred, own, pair, halo, far):
    ens, levels, width_x, width_y = shape
    pert, mean = centred
    vmem = pl.BlockSpec(memory_space=pltpu.VMEM)
    smem = pl.BlockSpec(memory_space=pltpu.SMEM)
    part = pl.pallas_call(
        functools.partial(inner_kernel, ens=ens, levels=levels, width_x=width_x),
        out_shape=jax.ShapeDtypeStruct((ens * (levels * width_x + SUB), width_y), F32),
        in_specs=[smem] + [vmem] * 5,
        out_specs=vmem,
        compiler_params=params(),
        cost_estimate=micros(3),
        name="inner",
    )(gz, pert, mean, own, pair, halo)
    return pl.pallas_call(
        outer_kernel,
        out_shape=jax.ShapeDtypeStruct(shape, BF16),
        in_specs=[smem] + [vmem] * 5,
        out_specs=vmem,
        scratch_shapes=[pltpu.VMEM((ens * (levels * width_x + SUB), width_y), F32)],
        compiler_params=params(),
        cost_estimate=micros(1),
        name="outer",
    )(gz, pert, mean, pair, far, part)


def shifted(x, axis, shift):
    size = lax.axis_size(axis)
    return lax.ppermute(x, axis, [((i + shift) % size, i) for i in range(size)])


def turned(x, shift):
    size = lax.axis_size("gx")
    pairs = [(2 * ((i + shift) % size), 2 * i) for i in range(size)]
    pairs += [(2 * ((i - shift) % size) + 1, 2 * i + 1) for i in range(size)]
    return lax.ppermute(x, ("gx", "gz"), pairs)


def swapped(x):
    return lax.ppermute(x, "gz", [(0, 1), (1, 0)])


def signed(index, count):
    return index if index <= count // 2 else index - count


def after(x, *others):
    return lax.optimization_barrier((x,) + others)[0]


def per_device(
    members, obs_value, obs_rinv, obs_count, stencil_cell, stencil_weight, patch_list, patch_taper
):
    ens = members.shape[0]
    slots = obs_value.shape[-1]
    _, patches, mloc = patch_list.shape
    size_x, size_y = lax.axis_size("gx"), lax.axis_size("gy")
    n_x, n_y = min(size_x, 5), min(size_y, 3)
    gz = lax.axis_index("gz").reshape(1).astype(jnp.int32)
    packet, sent, own_list = observe(
        gz,
        obs_count.reshape(1),
        members,
        stencil_cell.reshape(-1, slots),
        stencil_weight.reshape(-1, slots),
        obs_value.reshape(1, slots),
        obs_rinv.reshape(1, slots),
        jnp.swapaxes(patch_list, 1, 2),
        jnp.swapaxes(patch_taper, 1, 2),
    )
    rows = ens + SUB
    along = [packet] + [turned(packet, signed(x, n_x)) for x in range(1, n_x)]
    halo_list = turned(sent, -1)
    own_tapers = dense_tapers(gz, own_list, 0, patches, mloc, n_x, n_y, slots)
    along = jnp.stack(along, axis=0)
    centred = center(members)
    along = after(along, *own_tapers, *centred)
    beside = [shifted(along, "gy", signed(y, n_y)) for y in range(1, n_y)]
    halo_tapers = dense_tapers(gz, halo_list, -1, patches, mloc, n_x, n_y, slots)
    tapers = own_tapers + halo_tapers
    gram = grams(along, tapers, ens, range(n_x))
    here = jnp.concatenate([along] + after(beside, gram), axis=0)
    there = swapped(here)
    if n_y > 1:
        gram = grams(here[n_x:], tapers, ens, range(n_x, n_x * n_y), gram)
    gram = grams(there, tapers, ens, range(n_x * n_y, 2 * n_x * n_y), gram)
    own = roots(gram, 0, ens)
    pair = swapped(own)
    halo = roots(after(gram, own), 1, ens)
    far = swapped(halo)
    return update(gz, members.shape, centred, own, pair, halo, far)


def solution(mesh):
    return jax.shard_map(
        per_device,
        mesh=mesh,
        in_specs=(
            P("groups", "gz", "gx", "gy"),
            P(("groups", "gz"), "gx", "gy", None),
            P(("groups", "gz"), "gx", "gy", None),
            P(("groups", "gz"), "gx", "gy"),
            P(("groups", "gz"), "gx", "gy", None, None),
            P(("groups", "gz"), "gx", "gy", None, None),
            P(("groups", "gx"), "gy", None),
            P(("groups", "gx"), "gy", None),
        ),
        out_specs=P("groups", "gz", "gx", "gy"),
        check_vma=False,
    )
```

```python
import functools
import math

import jax
import jax.numpy as jnp
from jax import lax
from jax.experimental import pallas as pl
from jax.experimental.pallas import tpu as pltpu
from jax.sharding import PartitionSpec as P

PX = 4
PIT = 40
BATCH = 8
F32 = jnp.float32
BF16 = jnp.bfloat16
LANES = 128
SUB = 8
VMEM_LIMIT = 40 << 20
WHOLE_VMEM = (64 << 20) - (256 << 10)


def params(limit=VMEM_LIMIT):
    return pltpu.CompilerParams(vmem_limit_bytes=limit)


def micros(time):
    return pl.CostEstimate(flops=int(time * 1e9), bytes_accessed=int(time * 3e6), transcendentals=0)


def spread(ref, row):
    return ref[pl.ds(row, SUB, stride=0), :]


def block_base(ens):
    nb = ens // SUB
    base, at = [], 0
    for i in range(ens):
        base.append(at)
        at += SUB * (nb - i // SUB)
    return base, at


def observe_kernel(
    gz_ref, count_ref, members_in, cell_in, weight_in, value_in, rinv_in, ids_in, tapers_in,
    out_ref, sent_ref, own_ref,
    members_ref, cell_ref, weight_ref, value_ref, rinv_ref, ids_ref, tapers_ref, wx, pick, part, sems,
):
    ins = (cell_in, weight_in, members_in, value_in, rinv_in, ids_in, tapers_in)
    here = (cell_ref, weight_ref, members_ref, value_ref, rinv_ref, ids_ref, tapers_ref)
    copies = [pltpu.make_async_copy(src, dst, sems.at[n]) for n, (src, dst) in enumerate(zip(ins, here))]
    for copy in copies:
        copy.start()
    copies[0].wait()
    copies[1].wait()
    ens, levels, width_x, width_y = members_ref.shape
    slots = cell_ref.shape[1]
    sten = cell_ref.shape[0]
    cell = cell_ref[...]
    low = jnp.bitwise_and(cell, width_y - 1)
    high = lax.shift_right_logical(cell, width_y.bit_length() - 1)
    low0 = jnp.min(low, axis=0, keepdims=True)
    code = high * 2 + (low - low0)
    weight = weight_ref[...]
    x_iota = lax.broadcasted_iota(jnp.int32, (width_x, slots), 0)
    for level in range(levels):
        for c in range(2):
            want = (level * width_x + x_iota) * 2 + c
            total = jnp.zeros((width_x, slots), F32)
            for s in range(sten):
                total = total + jnp.where(code[s : s + 1] == want, weight[s : s + 1], 0.0)
            wx[c, level * width_x : (level + 1) * width_x, :] = total
    y_iota = lax.broadcasted_iota(jnp.int32, (width_y, slots), 0)
    pick[:, :slots] = jnp.where(y_iota == low0, 1.0, 0.0).astype(BF16)
    pick[:, slots:] = jnp.where(y_iota == low0 + 1, 1.0, 0.0).astype(BF16)
    for copy in copies[3:]:
        copy.wait()
    gz = gz_ref[0]
    own_ref[...] = jnp.concatenate([ids_ref[gz].astype(F32), tapers_ref[gz]], axis=0).T
    sent_ref[...] = jnp.concatenate([ids_ref[1 - gz].astype(F32), tapers_ref[1 - gz]], axis=0).T
    copies[2].wait()

    cells = levels * width_x

    def batch(step, _):
        rows = members_ref[pl.ds(step * BATCH, BATCH)].astype(F32).reshape(BATCH * cells, width_y).astype(BF16)
        got = jnp.dot(rows, pick[...], preferred_element_type=F32)
        for q in range(BATCH):
            total = None
            for at in range(0, cells, SUB):
                row = slice(q * cells + at, q * cells + at + SUB)
                near = slice(at, at + SUB)
                term = got[row, :slots] * wx[0, near] + got[row, slots:] * wx[1, near]
                total = term if at == 0 else total + term
            for half in range(slots // LANES):
                at = pl.ds(pl.multiple_of((step * BATCH + q) * SUB, SUB), SUB)
                part[half, at, :] = total[:, half * LANES : (half + 1) * LANES]
        return 0

    lax.fori_loop(0, ens // BATCH, batch, 0, unroll=True)
    groups = []
    for kb in range(ens // SUB):
        halves = []
        for half in range(slots // LANES):
            total = part[half, pl.ds(kb * SUB * SUB, SUB, stride=SUB), :]
            for s in range(1, SUB):
                total = total + part[half, pl.ds(kb * SUB * SUB + s, SUB, stride=SUB), :]
            halves.append(total)
        groups.append(jnp.concatenate(halves, axis=1))
    total = groups[0]
    for group in groups[1:]:
        total = total + group
    mean = jnp.sum(total, axis=0, keepdims=True) / ens
    for kb in range(ens // SUB):
        pert = groups[kb] - mean
        for half in range(slots // LANES):
            at = half * ens + kb * SUB
            out_ref[at : at + SUB, :] = pert[:, half * LANES : (half + 1) * LANES]
    live = lax.broadcasted_iota(jnp.int32, (1, slots), 1) < count_ref[0]
    innovation = value_ref[...] - mean
    rinv = jnp.where(live, rinv_ref[...], 0.0)
    row = lax.broadcasted_iota(jnp.int32, (SUB, LANES), 0)
    last = jnp.zeros((SUB, LANES), F32)
    for n, vector in enumerate((innovation, rinv)):
        for half in range(slots // LANES):
            lanes = vector[:, half * LANES : (half + 1) * LANES]
            last = jnp.where(row == n * (slots // LANES) + half, lanes, last)
    out_ref[slots // LANES * ens :, :] = last


def observe(gz, count, members, cell, weight, value, rinv, ids, tapers):
    ens, levels, width_x, width_y = members.shape
    sten, slots = cell.shape
    _, mloc, patches = ids.shape
    vmem = pl.BlockSpec(memory_space=pltpu.VMEM)
    smem = pl.BlockSpec(memory_space=pltpu.SMEM)
    return pl.pallas_call(
        observe_kernel,
        out_shape=(
            jax.ShapeDtypeStruct((slots // LANES * ens + SUB, LANES), F32),
            jax.ShapeDtypeStruct((patches, 2 * mloc), F32),
            jax.ShapeDtypeStruct((patches, 2 * mloc), F32),
        ),
        in_specs=[smem, smem] + [pl.BlockSpec(memory_space=pltpu.HBM)] * 7,
        out_specs=(vmem, vmem, vmem),
        scratch_shapes=[
            pltpu.VMEM(members.shape, members.dtype),
            pltpu.VMEM(cell.shape, cell.dtype),
            pltpu.VMEM(weight.shape, F32),
            pltpu.VMEM(value.shape, F32),
            pltpu.VMEM(rinv.shape, F32),
            pltpu.VMEM(ids.shape, ids.dtype),
            pltpu.VMEM(tapers.shape, F32),
            pltpu.VMEM((2, levels * width_x, slots), F32),
            pltpu.VMEM((width_y, 2 * slots), BF16),
            pltpu.VMEM((slots // LANES, ens * SUB, LANES), F32),
            pltpu.SemaphoreType.DMA((7,)),
        ],
        compiler_params=params(WHOLE_VMEM),
        cost_estimate=micros(3),
        name="observe",
    )(gz, count, members, cell, weight, value, rinv, ids, tapers)


def taper_kernel(gz_ref, list_ref, high_ref, low_ref, code_s, slot_s, taper_s, *, shift, n_x, n_y, slots, mloc):
    patches = high_ref.shape[1]
    batch = patches // SUB
    gz = gz_ref[0]
    n_buf = 2 * n_x * n_y
    lanes = SUB * mloc
    pairs = [list_ref[pl.ds(q, batch, stride=SUB), :] for q in range(SUB)]
    ids = jnp.concatenate([pair[:, :mloc] for pair in pairs], axis=1).astype(jnp.int32)
    taper = jnp.concatenate([pair[:, mloc:] for pair in pairs], axis=1)
    tile = lax.shift_right_logical(ids, slots.bit_length() - 1)
    upper = (tile >= 9).astype(jnp.int32)
    tile = tile - 9 * upper
    a = (tile >= 3).astype(jnp.int32) + (tile >= 6).astype(jnp.int32)
    b = tile - 3 * a
    other = jnp.where(upper == gz, 0, 1)
    x = jnp.where(gz == 0, a - 1, 1 - a) + shift
    x = lax.rem(jnp.where(other == 0, x, -x) + 2 * n_x, n_x)
    y = lax.rem(b - 1 + n_y, n_y)
    patch = lax.shift_right_logical(lax.broadcasted_iota(jnp.int32, ids.shape, 1), mloc.bit_length() - 1)
    code_s[...] = (((other * n_y + y) * n_x + x) * SUB + patch).astype(F32)
    slot_s[...] = jnp.bitwise_and(ids, slots - 1).astype(F32)
    taper_s[...] = taper
    code_iota = lax.broadcasted_iota(jnp.int32, (n_buf * SUB, lanes), 0).astype(F32).astype(BF16)
    slot_iota = lax.broadcasted_iota(jnp.int32, (slots, lanes), 0).astype(F32).astype(BF16)
    zero, one = jnp.zeros((), BF16), jnp.ones((), BF16)

    def dense(it):
        code = code_s[pl.ds(it, 1), :].astype(BF16)
        slot = slot_s[pl.ds(it, 1), :].astype(BF16)
        taper = taper_s[pl.ds(it, 1), :]
        coarse = taper.astype(BF16)
        fine = (taper - coarse.astype(F32)).astype(BF16)
        hit = code_iota == code
        left = jnp.concatenate([jnp.where(hit, coarse, zero), jnp.where(hit, fine, zero)], axis=0)
        right = jnp.where(slot_iota == slot, one, zero)
        both = lax.dot_general(left, right, (((1,), (1,)), ((), ())), preferred_element_type=F32)
        return both[: n_buf * SUB] + both[n_buf * SUB :]

    def body(it, _):
        first = dense(2 * it)
        second = dense(2 * it + 1)
        for n in range(n_buf):
            rows = slice(n * SUB, (n + 1) * SUB)
            block = jnp.concatenate([first[rows], second[rows]], axis=0)
            high = block.astype(BF16)
            at = pl.ds(pl.multiple_of(it * 2 * SUB, 2 * SUB), 2 * SUB)
            high_ref[n, at, :] = high
            low_ref[n, at, :] = (block - high.astype(F32)).astype(BF16)
        return 0

    lax.fori_loop(0, batch // 2, body, 0, unroll=True)


def dense_tapers(gz, lists, shift, patches, mloc, n_x, n_y, slots):
    vmem = pl.BlockSpec(memory_space=pltpu.VMEM)
    n_buf = 2 * n_x * n_y
    shape = jax.ShapeDtypeStruct((n_buf, patches, slots), BF16)
    batch = patches // SUB
    return pl.pallas_call(
        functools.partial(taper_kernel, shift=shift, n_x=n_x, n_y=n_y, slots=slots, mloc=mloc),
        out_shape=(shape, shape),
        in_specs=[pl.BlockSpec(memory_space=pltpu.SMEM), vmem],
        out_specs=(vmem, vmem),
        scratch_shapes=[
            pltpu.VMEM((batch, SUB * mloc), F32),
            pltpu.VMEM((batch, SUB * mloc), F32),
            pltpu.VMEM((batch, SUB * mloc), F32),
        ],
        compiler_params=params(),
        cost_estimate=micros(3),
        name="dense_tapers",
    )(gz, lists)


def gram_kernel(*refs, ens, bufs, carry):
    refs = list(refs)
    before = refs.pop(0) if carry else None
    stack, own_high, own_low, halo_high, halo_low, out_ref, z_s, zr_s = refs
    nb = ens // SUB
    base, tri = block_base(ens)
    rows = tri + ens
    nt = (((1,), (1,)), ((), ()))
    for t, n in enumerate(bufs):
        parts = zr_s.shape[1] // LANES
        ob = jnp.concatenate([stack[t, q * ens : (q + 1) * ens, :] for q in range(parts)], axis=1)
        wi, rinv = [
            jnp.concatenate([stack[t, ens * parts + n + q : ens * parts + n + q + 1, :] for q in range(parts)], axis=1)
            for n in (0, parts)
        ]
        zr_s[...] = ob * rinv
        for i in range(0, ens, 2):
            ib = i // SUB
            part = jnp.concatenate(
                [ob[kb * SUB : (kb + 1) * SUB] * zr_s[q : q + 1, :] for q in (i, i + 1) for kb in range(ib, nb)], axis=0
            )
            high = part.astype(BF16)
            z_s[base[i] : base[i] + part.shape[0], :] = high
            z_s[rows + base[i] : rows + base[i] + part.shape[0], :] = (part - high.astype(F32)).astype(BF16)
        part = zr_s[...] * wi
        high = part.astype(BF16)
        z_s[tri:rows, :] = high
        z_s[rows + tri : 2 * rows, :] = (part - high.astype(F32)).astype(BF16)
        right = jnp.concatenate([own_high[n], halo_high[n]], axis=0)
        got = lax.dot_general(z_s[...], right, nt, preferred_element_type=F32)
        right = jnp.concatenate([own_low[n], halo_low[n]], axis=0)
        more = lax.dot_general(z_s[:rows, :], right, nt, preferred_element_type=F32)
        total = got[:rows] + (got[rows:] + more)
        if t > 0:
            total = out_ref[...] + total
        elif carry:
            total = before[...] + total
        out_ref[...] = total


def grams(stack, tapers, ens, bufs, before=None):
    vmem = pl.BlockSpec(memory_space=pltpu.VMEM)
    _, tri = block_base(ens)
    rows = tri + ens
    _, patches, slots = tapers[0].shape
    carry = before is not None
    args = ((before,) if carry else ()) + (stack,) + tuple(tapers)
    return pl.pallas_call(
        functools.partial(gram_kernel, ens=ens, bufs=tuple(bufs), carry=carry),
        out_shape=jax.ShapeDtypeStruct((rows, 2 * patches), F32),
        in_specs=[vmem] * len(args),
        out_specs=vmem,
        scratch_shapes=[pltpu.VMEM((2 * rows, slots), BF16), pltpu.VMEM((ens, slots), F32)],
        compiler_params=params(),
        cost_estimate=micros(2),
        name="grams",
    )(*args)


def product(ens, a, b, dests, epilogue):
    nb = ens // SUB
    for ib in range(nb):
        n = nb - ib
        rows = 4 if n > 2 else 8

        def body(step, _, ib=ib, n=n, rows=rows):
            i0 = ib * SUB + step * rows
            acc = [[None] * n for _ in range(rows)]
            for j in range(ens):
                right = [b[j * PIT + SUB * kb : j * PIT + SUB * (kb + 1), :] for kb in range(ib, nb)]
                for ii in range(rows):
                    left = spread(a, (i0 + ii) * PIT + j)
                    for q in range(n):
                        term = left * right[q]
                        acc[ii][q] = term if j == 0 else acc[ii][q] + term
            for ii in range(rows):
                for q in range(n):
                    kb = ib + q
                    eye = None
                    if q == 0:
                        eye = lax.broadcasted_iota(jnp.int32, (SUB, LANES), 0) == step * rows + ii
                    outs = epilogue(acc[ii][q], pl.ds((i0 + ii) * PIT + SUB * kb, SUB), eye)
                    for dest, value in zip(dests, outs):
                        dest[pl.ds((i0 + ii) * PIT + SUB * kb, SUB), :] = value
                        if kb > ib:
                            dest[pl.ds(SUB * kb * PIT + i0 + ii, SUB, stride=PIT), :] = value
            return 0

        lax.fori_loop(0, SUB // rows, body, 0, unroll=True)


def root_kernel(gram_ref, out_ref, s_a, s_b, s_c, s_d, vec, *, ens, row):
    nb = ens // SUB
    base, tri = block_base(ens)
    lanes = slice(row * LANES, (row + 1) * LANES)
    diag = gram_ref[0:1, lanes]
    for i in range(1, ens):
        at = base[i] + i % SUB
        diag = diag + gram_ref[at : at + 1, lanes]
    half = 0.5 * (diag + (ens - 1.0) * ens)
    scale = jnp.broadcast_to(1.0 / half, (SUB, LANES))
    iota = lax.broadcasted_iota(jnp.int32, (SUB, LANES), 0)
    for i in range(ens):
        for kb in range(i // SUB, nb):
            at = base[i] + SUB * (kb - i // SUB)
            value = gram_ref[at : at + SUB, lanes]
            if kb == i // SUB:
                value = jnp.where(iota == i % SUB, value + (ens - 1.0), value)
            value = value * scale
            s_a[i * PIT + SUB * kb : i * PIT + SUB * (kb + 1), :] = value
            if kb > i // SUB:
                s_a[pl.ds(SUB * kb * PIT + i, SUB, stride=PIT), :] = value

    def plain(acc, at, eye):
        return (acc,)

    def quadratic(lin):
        def epilogue(acc, at, eye):
            rest = 0.0625 * acc - 0.5625 * lin[at, :]
            if eye is not None:
                rest = jnp.where(eye, rest + 1.6875, rest)
            return (acc, rest)

        return epilogue

    def quartic(lin):
        def epilogue(acc, at, eye):
            rest = acc - 2.4375 * lin[at, :]
            if eye is not None:
                rest = jnp.where(eye, rest + 2.25, rest)
            return (rest,)

        return epilogue

    product(ens, s_a, s_a, (s_b, s_c), quadratic(s_a))
    product(ens, s_b, s_c, (s_d,), quartic(s_a))
    product(ens, s_d, s_d, (s_b,), plain)
    product(ens, s_a, s_b, (s_c,), plain)
    product(ens, s_c, s_c, (s_a, s_b), quadratic(s_c))
    product(ens, s_a, s_b, (vec.at[pl.ds(0, ens * PIT)],), quartic(s_c))
    product(ens, s_d, vec.at[pl.ds(0, ens * PIT)], (s_a,), plain)

    right = ens * PIT
    vec[right : right + ens, :] = gram_ref[tri : tri + ens, lanes]

    def apply(source):
        sums = [None] * nb
        for i in range(ens):
            left = spread(vec, source + i)
            for kb in range(nb):
                term = left * s_a[i * PIT + SUB * kb : i * PIT + SUB * (kb + 1), :]
                sums[kb] = term if i == 0 else sums[kb] + term
        return sums

    inner = apply(right)
    for kb in range(nb):
        vec[right + ens + SUB * kb : right + ens + SUB * (kb + 1), :] = inner[kb]
    outer = apply(right + ens)
    for kb in range(nb):
        vec[right + SUB * kb : right + SUB * (kb + 1), :] = outer[kb] * scale
    factor = jnp.broadcast_to(math.sqrt(ens - 1.0) / jnp.sqrt(half), (SUB, LANES))
    for j in range(ens):
        weight = spread(vec, right + j)
        for kb in range(nb):
            at = slice(j * PIT + SUB * kb, j * PIT + SUB * (kb + 1))
            out_ref[j * ens + SUB * kb : j * ens + SUB * (kb + 1), :] = weight + s_a[at, :] * factor


def roots(gram, row, ens):
    square = pltpu.VMEM((ens * PIT, LANES), F32)
    vmem = pl.BlockSpec(memory_space=pltpu.VMEM)
    return pl.pallas_call(
        functools.partial(root_kernel, ens=ens, row=row),
        out_shape=jax.ShapeDtypeStruct((ens * ens, LANES), F32),
        in_specs=[vmem],
        out_specs=vmem,
        scratch_shapes=[square] * 4 + [pltpu.VMEM((ens * PIT + 2 * ens, LANES), F32)],
        compiler_params=params(),
        cost_estimate=micros(7),
        name="roots",
    )(gram)


def center_kernel(members_ref, pert_ref, mean_ref):
    ens, levels, width_x, _ = members_ref.shape
    for level in range(levels):
        total = members_ref[0, level].astype(F32)
        for k in range(1, ens):
            total = total + members_ref[k, level].astype(F32)
        mean = total / ens
        mean_ref[level * width_x : (level + 1) * width_x, :] = mean
        for k in range(ens):
            at = (k * levels + level) * width_x
            pert_ref[at : at + width_x, :] = members_ref[k, level].astype(F32) - mean


def center(members):
    ens, levels, width_x, width_y = members.shape
    vmem = pl.BlockSpec(memory_space=pltpu.VMEM)
    cells = levels * width_x
    return pl.pallas_call(
        center_kernel,
        out_shape=(
            jax.ShapeDtypeStruct((ens * cells, width_y), F32),
            jax.ShapeDtypeStruct((cells, width_y), F32),
        ),
        in_specs=[vmem],
        out_specs=(vmem, vmem),
        compiler_params=params(),
        cost_estimate=micros(1),
        name="center",
    )(members)


def columns(gz, pert_ref, mean_ref, dest, main_ref, beside_ref, first, ens, levels, width_x):
    nb = ens // SUB
    near = first % PX
    step_k = levels * width_x + SUB

    def body(step, _):
        place = jnp.abs((near + step + 0.5) / PX - 0.5)
        turned_x = first + step
        x = jnp.where(gz == 0, turned_x, width_x - 1 - turned_x)
        w_main = jnp.broadcast_to(1.0 - place, (SUB, LANES))
        w_beside = jnp.broadcast_to(place, (SUB, LANES))
        acc = [[spread(mean_ref, level * width_x + x)] * nb for level in range(levels)]
        for j in range(ens):
            blend = []
            for kb in range(nb):
                at = slice(j * ens + SUB * kb, j * ens + SUB * (kb + 1))
                blend.append(w_main * main_ref[at, :] + w_beside * beside_ref[at, :])
            for level in range(levels):
                pert = spread(pert_ref, (j * levels + level) * width_x + x)
                for kb in range(nb):
                    acc[level][kb] = acc[level][kb] + pert * blend[kb]
        for level in range(levels):
            for kb in range(nb):
                at = SUB * kb * step_k + level * width_x + x
                dest[pl.ds(at, SUB, stride=step_k), :] = acc[level][kb]
        return 0

    lax.fori_loop(0, PX // 2, body, 0)


def inner_kernel(gz_ref, pert_ref, mean_ref, own_ref, pair_ref, halo_ref, part_ref, *, ens, levels, width_x):
    gz = gz_ref[0]
    sizes = (ens, levels, width_x)
    columns(gz, pert_ref, mean_ref, part_ref, own_ref, halo_ref, 0, *sizes)
    columns(gz, pert_ref, mean_ref, part_ref, own_ref, pair_ref, PX // 2, *sizes)
    columns(gz, pert_ref, mean_ref, part_ref, pair_ref, own_ref, PX, *sizes)


def outer_kernel(gz_ref, pert_ref, mean_ref, pair_ref, far_ref, part_ref, out_hbm, rest_s, out_ref, sems):
    ens, levels, width_x, width_y = out_ref.shape
    gz = gz_ref[0]
    first = 3 * PX // 2
    step_k = levels * width_x + SUB
    columns(gz, pert_ref, mean_ref, rest_s, pair_ref, far_ref, first, ens, levels, width_x)
    x = lax.broadcasted_iota(jnp.int32, (width_x, width_y), 0)
    inside = jnp.where(gz == 0, x, width_x - 1 - x) < first
    copies = []
    for kb in range(ens // SUB):
        members = pl.ds(kb * SUB, SUB)
        for k in range(kb * SUB, (kb + 1) * SUB):
            for level in range(levels):
                at = slice(k * step_k + level * width_x, k * step_k + (level + 1) * width_x)
                out_ref[k, level] = jnp.where(inside, part_ref[at, :], rest_s[at, :]).astype(BF16)
        copies.append(pltpu.make_async_copy(out_ref.at[members], out_hbm.at[members], sems.at[kb]))
        copies[-1].start()
    for copy in copies:
        copy.wait()


def update(gz, shape, centred, own, pair, halo, far):
    ens, levels, width_x, width_y = shape
    pert, mean = centred
    vmem = pl.BlockSpec(memory_space=pltpu.VMEM)
    smem = pl.BlockSpec(memory_space=pltpu.SMEM)
    part = pl.pallas_call(
        functools.partial(inner_kernel, ens=ens, levels=levels, width_x=width_x),
        out_shape=jax.ShapeDtypeStruct((ens * (levels * width_x + SUB), width_y), F32),
        in_specs=[smem] + [vmem] * 5,
        out_specs=vmem,
        compiler_params=params(),
        cost_estimate=micros(3),
        name="inner",
    )(gz, pert, mean, own, pair, halo)
    return pl.pallas_call(
        outer_kernel,
        out_shape=jax.ShapeDtypeStruct(shape, BF16),
        in_specs=[smem] + [vmem] * 5,
        out_specs=pl.BlockSpec(memory_space=pltpu.HBM),
        scratch_shapes=[
            pltpu.VMEM((ens * (levels * width_x + SUB), width_y), F32),
            pltpu.VMEM(shape, BF16),
            pltpu.SemaphoreType.DMA((ens // SUB,)),
        ],
        compiler_params=params(),
        cost_estimate=micros(1),
        name="outer",
    )(gz, pert, mean, pair, far, part)


def shifted(x, axis, shift):
    size = lax.axis_size(axis)
    return lax.ppermute(x, axis, [((i + shift) % size, i) for i in range(size)])


def turned(x, shift):
    size = lax.axis_size("gx")
    pairs = [(2 * ((i + shift) % size), 2 * i) for i in range(size)]
    pairs += [(2 * ((i - shift) % size) + 1, 2 * i + 1) for i in range(size)]
    return lax.ppermute(x, ("gx", "gz"), pairs)


def swapped(x):
    return lax.ppermute(x, "gz", [(0, 1), (1, 0)])


def signed(index, count):
    return index if index <= count // 2 else index - count


def after(x, *others):
    return lax.optimization_barrier((x,) + others)[0]


def per_device(
    members, obs_value, obs_rinv, obs_count, stencil_cell, stencil_weight, patch_list, patch_taper
):
    ens = members.shape[0]
    slots = obs_value.shape[-1]
    _, patches, mloc = patch_list.shape
    size_x, size_y = lax.axis_size("gx"), lax.axis_size("gy")
    n_x, n_y = min(size_x, 5), min(size_y, 3)
    gz = lax.axis_index("gz").reshape(1).astype(jnp.int32)
    packet, sent, own_list = observe(
        gz,
        obs_count.reshape(1),
        members,
        stencil_cell.reshape(-1, slots),
        stencil_weight.reshape(-1, slots),
        obs_value.reshape(1, slots),
        obs_rinv.reshape(1, slots),
        jnp.swapaxes(patch_list, 1, 2),
        jnp.swapaxes(patch_taper, 1, 2),
    )
    along = [packet] + [turned(packet, signed(x, n_x)) for x in range(1, n_x)]
    halo_list = turned(sent, -1)
    own_tapers = dense_tapers(gz, own_list, 0, patches, mloc, n_x, n_y, slots)
    along = jnp.stack(along, axis=0)
    along = after(along, *own_tapers)
    beside = [shifted(along, "gy", signed(y, n_y)) for y in range(1, n_y)]
    centred = center(after(members, along))
    halo_tapers = dense_tapers(gz, halo_list, -1, patches, mloc, n_x, n_y, slots)
    tapers = own_tapers + halo_tapers
    gram = grams(along, tapers, ens, range(n_x))
    here = jnp.concatenate([along] + after(beside, gram, *centred), axis=0)
    there = swapped(here)
    if n_y > 1:
        gram = grams(here[n_x:], tapers, ens, range(n_x, n_x * n_y), gram)
    gram = grams(there, tapers, ens, range(n_x * n_y, 2 * n_x * n_y), gram)
    own = roots(gram, 0, ens)
    pair = swapped(own)
    halo = roots(after(gram, own), 1, ens)
    far = swapped(halo)
    return update(gz, members.shape, centred, own, pair, halo, far)


def solution(mesh):
    return jax.shard_map(
        per_device,
        mesh=mesh,
        in_specs=(
            P("groups", "gz", "gx", "gy"),
            P(("groups", "gz"), "gx", "gy", None),
            P(("groups", "gz"), "gx", "gy", None),
            P(("groups", "gz"), "gx", "gy"),
            P(("groups", "gz"), "gx", "gy", None, None),
            P(("groups", "gz"), "gx", "gy", None, None),
            P(("groups", "gx"), "gy", None),
            P(("groups", "gx"), "gy", None),
        ),
        out_specs=P("groups", "gz", "gx", "gy"),
        check_vma=False,
    )
```

```python
import functools
import math

import jax
import jax.numpy as jnp
from jax import lax
from jax.experimental import pallas as pl
from jax.experimental.pallas import tpu as pltpu
from jax.sharding import PartitionSpec as P

PX = 4
PIT = 40
BATCH = 16
F32 = jnp.float32
BF16 = jnp.bfloat16
LANES = 128
SUB = 8
VMEM_LIMIT = 40 << 20
WHOLE_VMEM = (64 << 20) - (256 << 10)


def params(limit=VMEM_LIMIT):
    return pltpu.CompilerParams(vmem_limit_bytes=limit)


def micros(time):
    return pl.CostEstimate(flops=int(time * 1e9), bytes_accessed=int(time * 3e6), transcendentals=0)


def spread(ref, row):
    return ref[pl.ds(row, SUB, stride=0), :]


def block_base(ens):
    nb = ens // SUB
    base, at = [], 0
    for i in range(ens):
        base.append(at)
        at += SUB * (nb - i // SUB)
    return base, at


def observe_kernel(
    gz_ref, count_ref, members_in, cell_in, weight_in, value_in, rinv_in, ids_in, tapers_in,
    out_ref, sent_ref, own_ref,
    members_ref, cell_ref, weight_ref, value_ref, rinv_ref, ids_ref, tapers_ref, wx, pick, part, sems,
):
    ins = (cell_in, weight_in, members_in, value_in, rinv_in, ids_in, tapers_in)
    here = (cell_ref, weight_ref, members_ref, value_ref, rinv_ref, ids_ref, tapers_ref)
    copies = [pltpu.make_async_copy(src, dst, sems.at[n]) for n, (src, dst) in enumerate(zip(ins, here))]
    for copy in copies:
        copy.start()
    copies[0].wait()
    copies[1].wait()
    ens, levels, width_x, width_y = members_ref.shape
    slots = cell_ref.shape[1]
    sten = cell_ref.shape[0]
    cell = cell_ref[...]
    low = jnp.bitwise_and(cell, width_y - 1)
    high = lax.shift_right_logical(cell, width_y.bit_length() - 1)
    low0 = jnp.min(low, axis=0, keepdims=True)
    code = high * 2 + (low - low0)
    weight = weight_ref[...]
    x_iota = lax.broadcasted_iota(jnp.int32, (width_x, slots), 0)
    for level in range(levels):
        for c in range(2):
            want = (level * width_x + x_iota) * 2 + c
            total = jnp.zeros((width_x, slots), F32)
            for s in range(sten):
                total = total + jnp.where(code[s : s + 1] == want, weight[s : s + 1], 0.0)
            wx[c, level * width_x : (level + 1) * width_x, :] = total
    y_iota = lax.broadcasted_iota(jnp.int32, (width_y, slots), 0)
    pick[:, :slots] = jnp.where(y_iota == low0, 1.0, 0.0).astype(BF16)
    pick[:, slots:] = jnp.where(y_iota == low0 + 1, 1.0, 0.0).astype(BF16)
    for copy in copies[3:]:
        copy.wait()
    gz = gz_ref[0]
    own_ref[...] = jnp.concatenate([ids_ref[gz].astype(F32), tapers_ref[gz]], axis=0).T
    sent_ref[...] = jnp.concatenate([ids_ref[1 - gz].astype(F32), tapers_ref[1 - gz]], axis=0).T
    copies[2].wait()

    cells = levels * width_x

    def batch(step, _):
        rows = members_ref[pl.ds(step * BATCH, BATCH)].astype(F32).reshape(BATCH * cells, width_y).astype(BF16)
        got = jnp.dot(rows, pick[...], preferred_element_type=F32)
        for q in range(BATCH):
            total = None
            for at in range(0, cells, SUB):
                row = slice(q * cells + at, q * cells + at + SUB)
                near = slice(at, at + SUB)
                term = got[row, :slots] * wx[0, near] + got[row, slots:] * wx[1, near]
                total = term if at == 0 else total + term
            for half in range(slots // LANES):
                at = pl.ds(pl.multiple_of((step * BATCH + q) * SUB, SUB), SUB)
                part[half, at, :] = total[:, half * LANES : (half + 1) * LANES]
        return 0

    lax.fori_loop(0, ens // BATCH, batch, 0, unroll=True)
    groups = []
    for kb in range(ens // SUB):
        halves = []
        for half in range(slots // LANES):
            total = part[half, pl.ds(kb * SUB * SUB, SUB, stride=SUB), :]
            for s in range(1, SUB):
                total = total + part[half, pl.ds(kb * SUB * SUB + s, SUB, stride=SUB), :]
            halves.append(total)
        groups.append(jnp.concatenate(halves, axis=1))
    total = groups[0]
    for group in groups[1:]:
        total = total + group
    mean = jnp.sum(total, axis=0, keepdims=True) / ens
    for kb in range(ens // SUB):
        pert = groups[kb] - mean
        for half in range(slots // LANES):
            at = half * ens + kb * SUB
            out_ref[at : at + SUB, :] = pert[:, half * LANES : (half + 1) * LANES]
    live = lax.broadcasted_iota(jnp.int32, (1, slots), 1) < count_ref[0]
    innovation = value_ref[...] - mean
    rinv = jnp.where(live, rinv_ref[...], 0.0)
    row = lax.broadcasted_iota(jnp.int32, (SUB, LANES), 0)
    last = jnp.zeros((SUB, LANES), F32)
    for n, vector in enumerate((innovation, rinv)):
        for half in range(slots // LANES):
            lanes = vector[:, half * LANES : (half + 1) * LANES]
            last = jnp.where(row == n * (slots // LANES) + half, lanes, last)
    out_ref[slots // LANES * ens :, :] = last


def observe(gz, count, members, cell, weight, value, rinv, ids, tapers):
    ens, levels, width_x, width_y = members.shape
    sten, slots = cell.shape
    _, mloc, patches = ids.shape
    vmem = pl.BlockSpec(memory_space=pltpu.VMEM)
    smem = pl.BlockSpec(memory_space=pltpu.SMEM)
    return pl.pallas_call(
        observe_kernel,
        out_shape=(
            jax.ShapeDtypeStruct((slots // LANES * ens + SUB, LANES), F32),
            jax.ShapeDtypeStruct((patches, 2 * mloc), F32),
            jax.ShapeDtypeStruct((patches, 2 * mloc), F32),
        ),
        in_specs=[smem, smem] + [pl.BlockSpec(memory_space=pltpu.HBM)] * 7,
        out_specs=(vmem, vmem, vmem),
        scratch_shapes=[
            pltpu.VMEM(members.shape, members.dtype),
            pltpu.VMEM(cell.shape, cell.dtype),
            pltpu.VMEM(weight.shape, F32),
            pltpu.VMEM(value.shape, F32),
            pltpu.VMEM(rinv.shape, F32),
            pltpu.VMEM(ids.shape, ids.dtype),
            pltpu.VMEM(tapers.shape, F32),
            pltpu.VMEM((2, levels * width_x, slots), F32),
            pltpu.VMEM((width_y, 2 * slots), BF16),
            pltpu.VMEM((slots // LANES, ens * SUB, LANES), F32),
            pltpu.SemaphoreType.DMA((7,)),
        ],
        compiler_params=params(WHOLE_VMEM),
        cost_estimate=micros(3),
        name="observe",
    )(gz, count, members, cell, weight, value, rinv, ids, tapers)


def taper_kernel(gz_ref, list_ref, high_ref, low_ref, code_s, slot_s, taper_s, *, shift, n_x, n_y, slots, mloc):
    patches = high_ref.shape[1]
    batch = patches // SUB
    gz = gz_ref[0]
    n_buf = 2 * n_x * n_y
    lanes = SUB * mloc
    pairs = [list_ref[pl.ds(q, batch, stride=SUB), :] for q in range(SUB)]
    ids = jnp.concatenate([pair[:, :mloc] for pair in pairs], axis=1).astype(jnp.int32)
    taper = jnp.concatenate([pair[:, mloc:] for pair in pairs], axis=1)
    tile = lax.shift_right_logical(ids, slots.bit_length() - 1)
    upper = (tile >= 9).astype(jnp.int32)
    tile = tile - 9 * upper
    a = (tile >= 3).astype(jnp.int32) + (tile >= 6).astype(jnp.int32)
    b = tile - 3 * a
    other = jnp.where(upper == gz, 0, 1)
    x = jnp.where(gz == 0, a - 1, 1 - a) + shift
    x = lax.rem(jnp.where(other == 0, x, -x) + 2 * n_x, n_x)
    y = lax.rem(b - 1 + n_y, n_y)
    patch = lax.shift_right_logical(lax.broadcasted_iota(jnp.int32, ids.shape, 1), mloc.bit_length() - 1)
    code_s[...] = (((other * n_y + y) * n_x + x) * SUB + patch).astype(F32)
    slot_s[...] = jnp.bitwise_and(ids, slots - 1).astype(F32)
    taper_s[...] = taper
    code_iota = lax.broadcasted_iota(jnp.int32, (n_buf * SUB, lanes), 0).astype(F32).astype(BF16)
    slot_iota = lax.broadcasted_iota(jnp.int32, (slots, lanes), 0).astype(F32).astype(BF16)
    zero, one = jnp.zeros((), BF16), jnp.ones((), BF16)

    def dense(it):
        code = code_s[pl.ds(it, 1), :].astype(BF16)
        slot = slot_s[pl.ds(it, 1), :].astype(BF16)
        taper = taper_s[pl.ds(it, 1), :]
        coarse = taper.astype(BF16)
        fine = (taper - coarse.astype(F32)).astype(BF16)
        hit = code_iota == code
        left = jnp.concatenate([jnp.where(hit, coarse, zero), jnp.where(hit, fine, zero)], axis=0)
        right = jnp.where(slot_iota == slot, one, zero)
        both = lax.dot_general(left, right, (((1,), (1,)), ((), ())), preferred_element_type=F32)
        return both[: n_buf * SUB] + both[n_buf * SUB :]

    def body(it, _):
        first = dense(2 * it)
        second = dense(2 * it + 1)
        for n in range(n_buf):
            rows = slice(n * SUB, (n + 1) * SUB)
            block = jnp.concatenate([first[rows], second[rows]], axis=0)
            high = block.astype(BF16)
            at = pl.ds(pl.multiple_of(it * 2 * SUB, 2 * SUB), 2 * SUB)
            high_ref[n, at, :] = high
            low_ref[n, at, :] = (block - high.astype(F32)).astype(BF16)
        return 0

    lax.fori_loop(0, batch // 2, body, 0, unroll=True)


def dense_tapers(gz, lists, shift, patches, mloc, n_x, n_y, slots):
    vmem = pl.BlockSpec(memory_space=pltpu.VMEM)
    n_buf = 2 * n_x * n_y
    shape = jax.ShapeDtypeStruct((n_buf, patches, slots), BF16)
    batch = patches // SUB
    return pl.pallas_call(
        functools.partial(taper_kernel, shift=shift, n_x=n_x, n_y=n_y, slots=slots, mloc=mloc),
        out_shape=(shape, shape),
        in_specs=[pl.BlockSpec(memory_space=pltpu.SMEM), vmem],
        out_specs=(vmem, vmem),
        scratch_shapes=[
            pltpu.VMEM((batch, SUB * mloc), F32),
            pltpu.VMEM((batch, SUB * mloc), F32),
            pltpu.VMEM((batch, SUB * mloc), F32),
        ],
        compiler_params=params(),
        cost_estimate=micros(3),
        name="dense_tapers",
    )(gz, lists)


def gram_kernel(*refs, ens, bufs, carry):
    refs = list(refs)
    before = refs.pop(0) if carry else None
    stack, own_high, own_low, halo_high, halo_low, out_ref, z_s, zr_s = refs
    nb = ens // SUB
    base, tri = block_base(ens)
    rows = tri + ens
    nt = (((1,), (1,)), ((), ()))
    for t, n in enumerate(bufs):
        parts = zr_s.shape[1] // LANES
        ob = jnp.concatenate([stack[t, q * ens : (q + 1) * ens, :] for q in range(parts)], axis=1)
        wi, rinv = [
            jnp.concatenate([stack[t, ens * parts + n + q : ens * parts + n + q + 1, :] for q in range(parts)], axis=1)
            for n in (0, parts)
        ]
        zr_s[...] = ob * rinv
        for i in range(0, ens, 2):
            ib = i // SUB
            part = jnp.concatenate(
                [ob[kb * SUB : (kb + 1) * SUB] * zr_s[q : q + 1, :] for q in (i, i + 1) for kb in range(ib, nb)], axis=0
            )
            high = part.astype(BF16)
            z_s[base[i] : base[i] + part.shape[0], :] = high
            z_s[rows + base[i] : rows + base[i] + part.shape[0], :] = (part - high.astype(F32)).astype(BF16)
        part = zr_s[...] * wi
        high = part.astype(BF16)
        z_s[tri:rows, :] = high
        z_s[rows + tri : 2 * rows, :] = (part - high.astype(F32)).astype(BF16)
        right = jnp.concatenate([own_high[n], halo_high[n]], axis=0)
        got = lax.dot_general(z_s[...], right, nt, preferred_element_type=F32)
        right = jnp.concatenate([own_low[n], halo_low[n]], axis=0)
        more = lax.dot_general(z_s[:rows, :], right, nt, preferred_element_type=F32)
        total = got[:rows] + (got[rows:] + more)
        if t > 0:
            total = out_ref[...] + total
        elif carry:
            total = before[...] + total
        out_ref[...] = total


def grams(stack, tapers, ens, bufs, before=None):
    vmem = pl.BlockSpec(memory_space=pltpu.VMEM)
    _, tri = block_base(ens)
    rows = tri + ens
    _, patches, slots = tapers[0].shape
    carry = before is not None
    args = ((before,) if carry else ()) + (stack,) + tuple(tapers)
    return pl.pallas_call(
        functools.partial(gram_kernel, ens=ens, bufs=tuple(bufs), carry=carry),
        out_shape=jax.ShapeDtypeStruct((rows, 2 * patches), F32),
        in_specs=[vmem] * len(args),
        out_specs=vmem,
        scratch_shapes=[pltpu.VMEM((2 * rows, slots), BF16), pltpu.VMEM((ens, slots), F32)],
        compiler_params=params(),
        cost_estimate=micros(2),
        name="grams",
    )(*args)


def product(ens, a, b, dests, epilogue):
    nb = ens // SUB
    for ib in range(nb):
        n = nb - ib
        rows = 4 if n > 2 else 8

        def body(step, _, ib=ib, n=n, rows=rows):
            i0 = ib * SUB + step * rows
            acc = [[None] * n for _ in range(rows)]
            for j in range(ens):
                right = [b[j * PIT + SUB * kb : j * PIT + SUB * (kb + 1), :] for kb in range(ib, nb)]
                for ii in range(rows):
                    left = spread(a, (i0 + ii) * PIT + j)
                    for q in range(n):
                        term = left * right[q]
                        acc[ii][q] = term if j == 0 else acc[ii][q] + term
            for ii in range(rows):
                for q in range(n):
                    kb = ib + q
                    eye = None
                    if q == 0:
                        eye = lax.broadcasted_iota(jnp.int32, (SUB, LANES), 0) == step * rows + ii
                    outs = epilogue(acc[ii][q], pl.ds((i0 + ii) * PIT + SUB * kb, SUB), eye)
                    for dest, value in zip(dests, outs):
                        dest[pl.ds((i0 + ii) * PIT + SUB * kb, SUB), :] = value
                        if kb > ib:
                            dest[pl.ds(SUB * kb * PIT + i0 + ii, SUB, stride=PIT), :] = value
            return 0

        lax.fori_loop(0, SUB // rows, body, 0, unroll=True)


def root_kernel(gram_ref, out_ref, s_a, s_b, s_c, s_d, vec, *, ens, row):
    nb = ens // SUB
    base, tri = block_base(ens)
    lanes = slice(row * LANES, (row + 1) * LANES)
    diag = gram_ref[0:1, lanes]
    for i in range(1, ens):
        at = base[i] + i % SUB
        diag = diag + gram_ref[at : at + 1, lanes]
    half = 0.5 * (diag + (ens - 1.0) * ens)
    scale = jnp.broadcast_to(1.0 / half, (SUB, LANES))
    iota = lax.broadcasted_iota(jnp.int32, (SUB, LANES), 0)
    for i in range(ens):
        for kb in range(i // SUB, nb):
            at = base[i] + SUB * (kb - i // SUB)
            value = gram_ref[at : at + SUB, lanes]
            if kb == i // SUB:
                value = jnp.where(iota == i % SUB, value + (ens - 1.0), value)
            value = value * scale
            s_a[i * PIT + SUB * kb : i * PIT + SUB * (kb + 1), :] = value
            if kb > i // SUB:
                s_a[pl.ds(SUB * kb * PIT + i, SUB, stride=PIT), :] = value

    def plain(acc, at, eye):
        return (acc,)

    def quadratic(lin):
        def epilogue(acc, at, eye):
            rest = 0.0625 * acc - 0.5625 * lin[at, :]
            if eye is not None:
                rest = jnp.where(eye, rest + 1.6875, rest)
            return (acc, rest)

        return epilogue

    def quartic(lin):
        def epilogue(acc, at, eye):
            rest = acc - 2.4375 * lin[at, :]
            if eye is not None:
                rest = jnp.where(eye, rest + 2.25, rest)
            return (rest,)

        return epilogue

    product(ens, s_a, s_a, (s_b, s_c), quadratic(s_a))
    product(ens, s_b, s_c, (s_d,), quartic(s_a))
    product(ens, s_d, s_d, (s_b,), plain)
    product(ens, s_a, s_b, (s_c,), plain)
    product(ens, s_c, s_c, (s_a, s_b), quadratic(s_c))
    product(ens, s_a, s_b, (vec.at[pl.ds(0, ens * PIT)],), quartic(s_c))
    product(ens, s_d, vec.at[pl.ds(0, ens * PIT)], (s_a,), plain)

    right = ens * PIT
    vec[right : right + ens, :] = gram_ref[tri : tri + ens, lanes]

    def apply(source):
        sums = [None] * nb
        for i in range(ens):
            left = spread(vec, source + i)
            for kb in range(nb):
                term = left * s_a[i * PIT + SUB * kb : i * PIT + SUB * (kb + 1), :]
                sums[kb] = term if i == 0 else sums[kb] + term
        return sums

    inner = apply(right)
    for kb in range(nb):
        vec[right + ens + SUB * kb : right + ens + SUB * (kb + 1), :] = inner[kb]
    outer = apply(right + ens)
    for kb in range(nb):
        vec[right + SUB * kb : right + SUB * (kb + 1), :] = outer[kb] * scale
    factor = jnp.broadcast_to(math.sqrt(ens - 1.0) / jnp.sqrt(half), (SUB, LANES))
    for j in range(ens):
        weight = spread(vec, right + j)
        for kb in range(nb):
            at = slice(j * PIT + SUB * kb, j * PIT + SUB * (kb + 1))
            out_ref[j * ens + SUB * kb : j * ens + SUB * (kb + 1), :] = weight + s_a[at, :] * factor


def roots(gram, row, ens):
    square = pltpu.VMEM((ens * PIT, LANES), F32)
    vmem = pl.BlockSpec(memory_space=pltpu.VMEM)
    return pl.pallas_call(
        functools.partial(root_kernel, ens=ens, row=row),
        out_shape=jax.ShapeDtypeStruct((ens * ens, LANES), F32),
        in_specs=[vmem],
        out_specs=vmem,
        scratch_shapes=[square] * 4 + [pltpu.VMEM((ens * PIT + 2 * ens, LANES), F32)],
        compiler_params=params(),
        cost_estimate=micros(7),
        name="roots",
    )(gram)


def center_kernel(members_ref, pert_ref, mean_ref):
    ens, levels, width_x, _ = members_ref.shape
    for level in range(levels):
        total = members_ref[0, level].astype(F32)
        for k in range(1, ens):
            total = total + members_ref[k, level].astype(F32)
        mean = total / ens
        mean_ref[level * width_x : (level + 1) * width_x, :] = mean
        for k in range(ens):
            at = (k * levels + level) * width_x
            pert_ref[at : at + width_x, :] = members_ref[k, level].astype(F32) - mean


def center(members):
    ens, levels, width_x, width_y = members.shape
    vmem = pl.BlockSpec(memory_space=pltpu.VMEM)
    cells = levels * width_x
    return pl.pallas_call(
        center_kernel,
        out_shape=(
            jax.ShapeDtypeStruct((ens * cells, width_y), F32),
            jax.ShapeDtypeStruct((cells, width_y), F32),
        ),
        in_specs=[vmem],
        out_specs=(vmem, vmem),
        compiler_params=params(),
        cost_estimate=micros(1),
        name="center",
    )(members)


def columns(gz, pert_ref, mean_ref, dest, main_ref, beside_ref, first, ens, levels, width_x):
    nb = ens // SUB
    near = first % PX
    step_k = levels * width_x + SUB

    def body(step, _):
        place = jnp.abs((near + step + 0.5) / PX - 0.5)
        turned_x = first + step
        x = jnp.where(gz == 0, turned_x, width_x - 1 - turned_x)
        w_main = jnp.broadcast_to(1.0 - place, (SUB, LANES))
        w_beside = jnp.broadcast_to(place, (SUB, LANES))
        acc = [[spread(mean_ref, level * width_x + x)] * nb for level in range(levels)]
        for j in range(ens):
            blend = []
            for kb in range(nb):
                at = slice(j * ens + SUB * kb, j * ens + SUB * (kb + 1))
                blend.append(w_main * main_ref[at, :] + w_beside * beside_ref[at, :])
            for level in range(levels):
                pert = spread(pert_ref, (j * levels + level) * width_x + x)
                for kb in range(nb):
                    acc[level][kb] = acc[level][kb] + pert * blend[kb]
        for level in range(levels):
            for kb in range(nb):
                at = SUB * kb * step_k + level * width_x + x
                dest[pl.ds(at, SUB, stride=step_k), :] = acc[level][kb]
        return 0

    lax.fori_loop(0, PX // 2, body, 0)


def inner_kernel(gz_ref, pert_ref, mean_ref, own_ref, pair_ref, halo_ref, part_ref, *, ens, levels, width_x):
    gz = gz_ref[0]
    sizes = (ens, levels, width_x)
    columns(gz, pert_ref, mean_ref, part_ref, own_ref, halo_ref, 0, *sizes)
    columns(gz, pert_ref, mean_ref, part_ref, own_ref, pair_ref, PX // 2, *sizes)
    columns(gz, pert_ref, mean_ref, part_ref, pair_ref, own_ref, PX, *sizes)


def outer_kernel(gz_ref, pert_ref, mean_ref, pair_ref, far_ref, part_ref, out_hbm, rest_s, out_ref, sems):
    ens, levels, width_x, width_y = out_ref.shape
    gz = gz_ref[0]
    first = 3 * PX // 2
    step_k = levels * width_x + SUB
    columns(gz, pert_ref, mean_ref, rest_s, pair_ref, far_ref, first, ens, levels, width_x)
    x = lax.broadcasted_iota(jnp.int32, (width_x, width_y), 0)
    inside = jnp.where(gz == 0, x, width_x - 1 - x) < first
    copies = []
    for kb in range(ens // SUB):
        members = pl.ds(kb * SUB, SUB)
        for k in range(kb * SUB, (kb + 1) * SUB):
            for level in range(levels):
                at = slice(k * step_k + level * width_x, k * step_k + (level + 1) * width_x)
                out_ref[k, level] = jnp.where(inside, part_ref[at, :], rest_s[at, :]).astype(BF16)
        copies.append(pltpu.make_async_copy(out_ref.at[members], out_hbm.at[members], sems.at[kb]))
        copies[-1].start()
    for copy in copies:
        copy.wait()


def update(gz, shape, centred, own, pair, halo, far):
    ens, levels, width_x, width_y = shape
    pert, mean = centred
    vmem = pl.BlockSpec(memory_space=pltpu.VMEM)
    smem = pl.BlockSpec(memory_space=pltpu.SMEM)
    part = pl.pallas_call(
        functools.partial(inner_kernel, ens=ens, levels=levels, width_x=width_x),
        out_shape=jax.ShapeDtypeStruct((ens * (levels * width_x + SUB), width_y), F32),
        in_specs=[smem] + [vmem] * 5,
        out_specs=vmem,
        compiler_params=params(),
        cost_estimate=micros(3),
        name="inner",
    )(gz, pert, mean, own, pair, halo)
    return pl.pallas_call(
        outer_kernel,
        out_shape=jax.ShapeDtypeStruct(shape, BF16),
        in_specs=[smem] + [vmem] * 5,
        out_specs=pl.BlockSpec(memory_space=pltpu.HBM),
        scratch_shapes=[
            pltpu.VMEM((ens * (levels * width_x + SUB), width_y), F32),
            pltpu.VMEM(shape, BF16),
            pltpu.SemaphoreType.DMA((ens // SUB,)),
        ],
        compiler_params=params(),
        cost_estimate=micros(1),
        name="outer",
    )(gz, pert, mean, pair, far, part)


def shifted(x, axis, shift):
    size = lax.axis_size(axis)
    return lax.ppermute(x, axis, [((i + shift) % size, i) for i in range(size)])


def turned(x, shift):
    size = lax.axis_size("gx")
    pairs = [(2 * ((i + shift) % size), 2 * i) for i in range(size)]
    pairs += [(2 * ((i - shift) % size) + 1, 2 * i + 1) for i in range(size)]
    return lax.ppermute(x, ("gx", "gz"), pairs)


def swapped(x):
    return lax.ppermute(x, "gz", [(0, 1), (1, 0)])


def signed(index, count):
    return index if index <= count // 2 else index - count


def after(x, *others):
    return lax.optimization_barrier((x,) + others)[0]


def per_device(
    members, obs_value, obs_rinv, obs_count, stencil_cell, stencil_weight, patch_list, patch_taper
):
    ens = members.shape[0]
    slots = obs_value.shape[-1]
    _, patches, mloc = patch_list.shape
    size_x, size_y = lax.axis_size("gx"), lax.axis_size("gy")
    n_x, n_y = min(size_x, 5), min(size_y, 3)
    gz = lax.axis_index("gz").reshape(1).astype(jnp.int32)
    packet, sent, own_list = observe(
        gz,
        obs_count.reshape(1),
        members,
        stencil_cell.reshape(-1, slots),
        stencil_weight.reshape(-1, slots),
        obs_value.reshape(1, slots),
        obs_rinv.reshape(1, slots),
        jnp.swapaxes(patch_list, 1, 2),
        jnp.swapaxes(patch_taper, 1, 2),
    )
    along = [packet] + [turned(packet, signed(x, n_x)) for x in range(1, n_x)]
    halo_list = turned(sent, -1)
    own_tapers = dense_tapers(gz, own_list, 0, patches, mloc, n_x, n_y, slots)
    along = jnp.stack(along, axis=0)
    along = after(along, *own_tapers)
    beside = [shifted(along, "gy", signed(y, n_y)) for y in range(1, n_y)]
    centred = center(after(members, along))
    halo_tapers = dense_tapers(gz, halo_list, -1, patches, mloc, n_x, n_y, slots)
    tapers = own_tapers + halo_tapers
    gram = grams(along, tapers, ens, range(n_x))
    here = jnp.concatenate([along] + after(beside, gram, *centred), axis=0)
    there = swapped(here)
    if n_y > 1:
        gram = grams(here[n_x:], tapers, ens, range(n_x, n_x * n_y), gram)
    gram = grams(there, tapers, ens, range(n_x * n_y, 2 * n_x * n_y), gram)
    own = roots(gram, 0, ens)
    pair = swapped(own)
    halo = roots(after(gram, own), 1, ens)
    far = swapped(halo)
    return update(gz, members.shape, centred, own, pair, halo, far)


def solution(mesh):
    return jax.shard_map(
        per_device,
        mesh=mesh,
        in_specs=(
            P("groups", "gz", "gx", "gy"),
            P(("groups", "gz"), "gx", "gy", None),
            P(("groups", "gz"), "gx", "gy", None),
            P(("groups", "gz"), "gx", "gy"),
            P(("groups", "gz"), "gx", "gy", None, None),
            P(("groups", "gz"), "gx", "gy", None, None),
            P(("groups", "gx"), "gy", None),
            P(("groups", "gx"), "gy", None),
        ),
        out_specs=P("groups", "gz", "gx", "gy"),
        check_vma=False,
    )
```
